128 devices in a mesh: dp: 8 (over y, core), mp: 16 (over x, z).
Axes of the slice: x: 4, y: 4, z: 4, core: 2. Of those that a mesh axis runs over, the one named last changes fastest.
Arguments:
- query_rows: bfloat16 [32768, 16, 128], P('dp', 'mp'), may hold values from -8 to 8
- key_rows: bfloat16 [32768, 16, 128], P('dp', 'mp'), may hold values from -8 to 8
- value_rows: bfloat16 [32768, 16, 128], P('dp', 'mp'), may hold values from -6 to 6
- residual: bfloat16 [16384, 16, 384], P('dp', 'mp'), may hold values from -40 to 40
- lengths: int32 [256], replicated, may hold values from 1 to 256, as said below
- assignment: int32 [256], replicated, may hold values from 0 to 7, as said below
- out_proj: bfloat16 [1024, 1536], P(None, 'mp'), may hold values from -0.1875 to 0.1875
- norm_gain: float32 [1536], replicated, may hold values from 0.5 to 1.5
- norm_bias: float32 [1536], replicated, may hold values from -3 to 3
- glu_proj: bfloat16 [1536, 3072], P(None, 'mp'), may hold values from -0.15625 to 0.15625
- conv_taps: float32 [31, 1536], replicated, may hold values from -1 to 1
- batch_scale: float32 [1536], replicated, may hold values from 0.25 to 1.75
- batch_shift: float32 [1536], replicated, may hold values from -3 to 3
- down_proj: bfloat16 [1536, 1536], P(None, 'mp'), may hold values from -0.15625 to 0.15625
Outputs:
- encoded: bfloat16 [65536, 1536], P(('dp', 'mp'))
The draws below stay inside these ranges and needn't reach their ends.
Inputs may be any that keep to these rules, and one draw needn't show every extreme that they name: `lengths`: utterance u starts in data group u // 32; a data group holds its utterances in order of u from its first frame on, and its frames after them are padding. In every draw every data group sends exactly 256 frames in each of its 4 utterances to one and the same data group, so that this group receives 4 * 256 frames from every data group; the utterances one data group sends to one data group never have more frames together. `assignment`: every data group sends exactly 4 of its utterances to each data group, itself included. In its new group an utterance lies after those of lower number, from the first frame on, and the frames after them are padding.
All inputs are finite; a program needn't handle non-finite values.
Results may differ from the reference program's by a relative error of at most 0.0034.
Values may be sent and summed in bfloat16 or wider, within the bound.
No kernel may reach another device: no remote copies, remote signals or barrier semaphores. Data moves between devices by JAX's collectives and lax.ppermute only.
A program may use at most 128 MiB of HBM per device.

```python
import math
import jax
import jax.numpy as jnp
from jax import lax

D = 1536
HEADS = 16
HD = 64
KERNEL = 31
HALF = 15
MAXLEN = 256
PIECES = 4
QBLK = 512
FEAT_DEV = 96
ROWS_G = 8192
ROWS = 65536
UTT_G = 32
UTTS = 256
N_DP = 8


def routing_tables(key):
    groups = UTTS // UTT_G
    routing_key = jax.random.fold_in(key, 7001)
    order_keys = jax.random.split(jax.random.fold_in(routing_key, 1), groups)
    orders = jax.vmap(lambda order_key: jax.random.permutation(order_key, UTT_G))(order_keys)
    targets = (orders // PIECES).reshape(UTTS).astype(jnp.int32)
    factor = jax.random.randint(jax.random.fold_in(routing_key, 2), (groups,), 1, 5)
    spread = jax.random.randint(jax.random.fold_in(routing_key, 3), (UTTS,), MAXLEN // 4, MAXLEN // 2 + 1)
    owner_group = jnp.arange(UTTS) // UTT_G
    spans_drawn = jnp.minimum(MAXLEN, factor[owner_group] * spread // 2)
    filled_group = jax.random.randint(jax.random.fold_in(routing_key, 4), (), 0, groups)
    heavy_group = (filled_group + 1) % groups
    spans_drawn = jnp.where(targets == heavy_group, MAXLEN - 1, spans_drawn)
    spans_drawn = jnp.where(targets == filled_group, MAXLEN, spans_drawn).astype(jnp.int32)
    return (spans_drawn, targets)


def draw_lengths(key, part):
    return routing_tables(key)[0]


def draw_assignment(key, part):
    return routing_tables(key)[1]


def pack_pairs(flat):
    return flat.reshape(ROWS // 2, 2, HEADS, HD).transpose(0, 2, 1, 3).reshape(ROWS // 2, HEADS, 2 * HD)


def drawn_pair(key):
    shape = (ROWS, HEADS * HD)
    query_key = jax.random.fold_in(key, 501)
    keys_key = jax.random.fold_in(key, 502)
    queries = jax.random.truncated_normal(query_key, -4.0, 4.0, shape, jnp.float32)
    keyset = jax.random.truncated_normal(keys_key, -4.0, 4.0, shape, jnp.float32)
    return (queries, keyset)


def draw_query_rows(key, part):
    return pack_pairs(drawn_pair(key)[0]).astype(jnp.bfloat16)


def draw_key_rows(key, part):
    return pack_pairs(drawn_pair(key)[1]).astype(jnp.bfloat16)


def draw_residual(key, part):
    row_scale = 0.3 * jnp.exp(jax.random.uniform(jax.random.fold_in(key, 601), (ROWS, 1), jnp.float32, 0.0, math.log(10.0)))
    column_scale = 0.3 * jnp.exp(jax.random.uniform(jax.random.fold_in(key, 602), (1, D), jnp.float32, 0.0, math.log(10.0)))
    basis = jax.random.truncated_normal(jax.random.fold_in(key, 605), -4.0, 4.0, (ROWS, D), jnp.float32)
    flat = basis * row_scale * column_scale
    blocks = D // FEAT_DEV
    packed = flat.reshape(ROWS // 4, 4, blocks, FEAT_DEV).transpose(0, 2, 1, 3).reshape(ROWS // 4, blocks, 4 * FEAT_DEV)
    return packed.astype(jnp.bfloat16)


def levels(rng, shape, shards, smallest, high):
    gain, own = 1.0, jax.random.fold_in(rng, 6)
    for dim, shards_of in shards:
        steps = jnp.exp(jax.random.uniform(jax.random.fold_in(own, dim), (shards_of,), jnp.float32, smallest / len(shards), high / len(shards)))
        gain = gain * jnp.repeat(steps, shape[dim] // shards_of).reshape([-1 if axis == dim else 1 for axis in range(len(shape))])
    return gain


def bell_draw(stream_key, extent, deviation, most, pieces=(), held_as=jnp.bfloat16):
    values = jax.random.normal(stream_key, extent, jnp.float32) * deviation
    if len(pieces) > 0:
        values = levels(stream_key, extent, pieces, -0.22, 0.18) * values
    return jnp.clip(values, min=-most, max=most).astype(held_as)


def setup_inputs(seed: int = 0) -> dict:
    seeds = jax.random.split(jax.random.key(seed), 15)
    query_rows = draw_query_rows(jax.random.fold_in(seeds[14], 71), 0)
    key_rows = draw_key_rows(jax.random.fold_in(seeds[14], 71), 0)
    value_rows = bell_draw(seeds[2], (ROWS // 2, HEADS, 2 * HD), 1.0, 6.0, ((0, 8), (1, 16)))
    residual = draw_residual(jax.random.fold_in(seeds[14], 71), 0)
    lengths = draw_lengths(jax.random.fold_in(seeds[14], 71), 0)
    assignment = draw_assignment(jax.random.fold_in(seeds[14], 71), 0)
    out_proj = bell_draw(seeds[6], (HEADS * HD, D), (HEADS * HD) ** -0.5, 0.1875, ((1, 16),))
    norm_gain = jnp.clip(1.0 + 0.1 * jax.random.normal(seeds[7], (D,), jnp.float32), 0.5, 1.5)
    norm_bias = bell_draw(seeds[8], (D,), 0.5, 3.0, (), jnp.float32)
    glu_proj = bell_draw(seeds[9], (D, 2 * D), D ** -0.5, 0.15625, ((1, 16),))
    conv_taps = bell_draw(seeds[10], (KERNEL, D), KERNEL ** -0.5, 1.0, (), jnp.float32)
    batch_scale = jnp.clip(1.0 + 0.15 * jax.random.normal(seeds[11], (D,), jnp.float32), 0.25, 1.75)
    batch_shift = bell_draw(seeds[12], (D,), 0.5, 3.0, (), jnp.float32)
    down_proj = bell_draw(seeds[13], (D, D), D ** -0.5, 0.15625, ((1, 16),))
    return dict(query_rows=query_rows, key_rows=key_rows, value_rows=value_rows, residual=residual, lengths=lengths, assignment=assignment, out_proj=out_proj, norm_gain=norm_gain, norm_bias=norm_bias, glu_proj=glu_proj, conv_taps=conv_taps, batch_scale=batch_scale, batch_shift=batch_shift, down_proj=down_proj)


EPS = 1e-05
MASKED = -1e+30

def unpack_pairs(packed):
    pair_rows, head_count, pair_width = packed.shape
    width = pair_width // 2
    return packed.reshape(pair_rows, head_count, 2, width).transpose(0, 2, 1, 3).reshape(pair_rows * 2, head_count * width)

def unpack_fours(packed):
    four_rows, block_count, four_width = packed.shape
    width = four_width // 4
    return packed.reshape(four_rows, block_count, 4, width).transpose(0, 2, 1, 3).reshape(four_rows * 4, block_count * width)

def utterance_tables(lengths, assignment):
    utterance = jnp.arange(UTTS, dtype=jnp.int32)
    source = utterance // UTT_G
    earlier = utterance[None, :] < utterance[:, None]
    same_source = source[None, :] == source[:, None]
    same_target = assignment[None, :] == assignment[:, None]
    span_table = jnp.broadcast_to(lengths[None, :], (UTTS, UTTS))
    nothing = jnp.zeros_like(span_table)
    before_start = lax.optimization_barrier(jnp.sum(jnp.where(earlier & same_source, span_table, nothing), axis=1))
    after_start = lax.optimization_barrier(jnp.sum(jnp.where(earlier & same_target, span_table, nothing), axis=1))
    return (source, before_start, after_start)

def find_frames(data_group, owner_group, first_frame, lengths, frames, lookup):
    position = jnp.arange(frames, dtype=jnp.int32)[:, None]
    matches = (owner_group[None, :] == data_group) & (position >= first_frame[None, :]) & (position < first_frame[None, :] + lengths[None, :])
    utterance = jnp.arange(lengths.shape[0], dtype=jnp.int32)[None, :]
    occupied_slots = jnp.any(matches, axis=1)
    segment = jnp.where(occupied_slots, lax.optimization_barrier(jnp.sum(jnp.where(matches, utterance, 0), axis=1)), -1).astype(jnp.int32)
    shifted = lax.optimization_barrier(jnp.sum(jnp.where(matches, lookup[None, :] - first_frame[None, :], 0), axis=1))
    source_row = jnp.where(occupied_slots, jnp.arange(frames, dtype=jnp.int32) + shifted, 0).astype(jnp.int32)
    return (segment, occupied_slots, source_row)

def attend(query_rows, key_rows, value_rows, segment):
    group_rows, width_per_head = query_rows.shape
    head_count = width_per_head // HD
    window = QBLK + 2 * MAXLEN
    score_scale = HD ** (-0.5)
    queries = query_rows.reshape(group_rows, head_count, HD).astype(jnp.float32)
    keyset = key_rows.reshape(group_rows, head_count, HD).astype(jnp.float32)
    valueset = value_rows.reshape(group_rows, head_count, HD).astype(jnp.float32)

    def attend_block(block_index, context):
        first_row = (block_index * QBLK).astype(jnp.int32)
        window_low = jnp.clip(first_row - MAXLEN, 0, group_rows - window).astype(jnp.int32)
        query_block = lax.dynamic_slice_in_dim(queries, first_row, QBLK, 0)
        key_block = lax.dynamic_slice_in_dim(keyset, window_low, window, 0)
        value_block = lax.dynamic_slice_in_dim(valueset, window_low, window, 0)
        segment_query = lax.dynamic_slice_in_dim(segment, first_row, QBLK, 0)
        segment_key = lax.dynamic_slice_in_dim(segment, window_low, window, 0)
        allowed = (segment_query[:, None] == segment_key[None, :]) & (segment_key[None, :] >= 0)
        scores = jnp.einsum('qhd,khd->hqk', query_block, key_block) * score_scale
        scores = jnp.where(allowed[None], scores, MASKED)
        highest = lax.optimization_barrier(jnp.max(scores, axis=2, keepdims=True))
        exponentials = jnp.exp(scores - highest)
        denominator = lax.optimization_barrier(jnp.sum(exponentials, axis=2, keepdims=True))
        weights = (exponentials / denominator).astype(jnp.bfloat16)
        blended = jnp.einsum('hqk,khd->qhd', weights.astype(jnp.float32), value_block)
        blended = jnp.where((segment_query >= 0)[:, None, None], blended, 0.0).astype(jnp.bfloat16)
        return lax.dynamic_update_slice_in_dim(context, blended.reshape(QBLK, width_per_head), first_row, 0)
    return lax.fori_loop(0, group_rows // QBLK, attend_block, jnp.zeros((group_rows, width_per_head), jnp.bfloat16))

def depthwise(gated_rows, segment, conv_taps):
    output_rows = gated_rows.shape[0] - 2 * HALF
    centre = segment[HALF:HALF + output_rows]
    accumulated = jnp.zeros((output_rows, gated_rows.shape[1]), jnp.float32)
    for tap_index in range(KERNEL):
        same_segment = (segment[tap_index:tap_index + output_rows] == centre)[:, None]
        term = jnp.where(same_segment, gated_rows[tap_index:tap_index + output_rows].astype(jnp.float32), 0.0)
        accumulated = accumulated + term * conv_taps[tap_index]
    return accumulated

def reference(query_rows, key_rows, value_rows, residual, lengths, assignment, out_proj, norm_gain, norm_bias, glu_proj, conv_taps, batch_scale, batch_shift, down_proj):
    query_flat = unpack_pairs(query_rows)
    key_flat = unpack_pairs(key_rows)
    value_flat = unpack_pairs(value_rows)
    residual_flat = unpack_fours(residual)
    source, before_start, after_start = utterance_tables(lengths, assignment)
    lookup = source * ROWS_G + before_start

    def one_group(data_group):
        segment, occupied_slots, source_row = find_frames(data_group, assignment, after_start, lengths, ROWS_G, lookup)

        def bring(array):
            picked = jnp.take(array, source_row, axis=0)
            return jnp.where(occupied_slots[:, None], picked, jnp.zeros((), array.dtype))
        context = attend(bring(query_flat), bring(key_flat), bring(value_flat), segment)
        carried = bring(residual_flat).astype(jnp.float32) + jnp.dot(context, out_proj, preferred_element_type=jnp.float32)
        average = lax.optimization_barrier(jnp.mean(carried, axis=1, keepdims=True))
        centred = carried - average
        variance = lax.optimization_barrier(jnp.mean(centred * centred, axis=1, keepdims=True))
        normed = (centred * lax.rsqrt(variance + EPS) * norm_gain + norm_bias).astype(jnp.bfloat16)
        halves = jnp.dot(normed, glu_proj, preferred_element_type=jnp.float32)
        gated_rows = (halves[:, :D] * jax.nn.sigmoid(halves[:, D:])).astype(jnp.bfloat16)
        padded = jnp.pad(gated_rows, ((HALF, HALF), (0, 0)))
        wide_segment = jnp.pad(segment, (HALF, HALF), constant_values=-2)
        convolved = depthwise(padded, wide_segment, conv_taps)
        affine = convolved * batch_scale + batch_shift
        swished = (affine * jax.nn.sigmoid(affine)).astype(jnp.bfloat16)
        lowered = jnp.dot(swished, down_proj, preferred_element_type=jnp.float32)
        return jnp.where((segment >= 0)[:, None], carried + lowered, 0.0).astype(jnp.bfloat16)
    encoded = lax.map(one_group, jnp.arange(N_DP, dtype=jnp.int32))
    return encoded.reshape(ROWS, D)
```

```python
import functools

import jax
import jax.numpy as jnp
from jax import lax
from jax.experimental import pallas as pl
from jax.experimental.pallas import tpu as pltpu
from jax.sharding import PartitionSpec as P

HD = 64
KERNEL = 31
HALF = 15
MAXLEN = 256
EPS = 1e-05
MASKED = -1e30

CELL = MAXLEN // 4
F32 = jnp.float32
BF16 = jnp.bfloat16
NT = (((1,), (1,)), ((), ()))


def cell_tables(data_group, lengths_ref, assignment_ref, start_ref, size_ref, seen_ref):
    per_group = 32
    for t in range(8):
        seen_ref[t] = 0

    def step(i, at):
        u = data_group * per_group + i
        t = assignment_ref[u]
        n = lengths_ref[u]
        k = seen_ref[t]
        seen_ref[t] = k + 1
        start_ref[4 * t + k] = at
        size_ref[4 * t + k] = n
        return at + n

    lax.fori_loop(0, per_group, step, jnp.int32(0))


def pack_kernel(group_ref, lengths_ref, assignment_ref, x_ref, o_ref, flat, start_ref, size_ref, seen_ref):
    cell_tables(group_ref[0], lengths_ref, assignment_ref, start_ref, size_ref, seen_ref)
    rows = x_ref.shape[0]

    def widen(i, _):
        r = pl.multiple_of(i * 64, 64)
        for b in range(3):
            flat[b, pl.ds(r, 64), :] = x_ref[pl.ds(r, 64), 128 * b : 128 * b + 128].astype(F32)
        return 0

    lax.fori_loop(0, rows // 64, widen, 0)
    for b in range(3):
        flat[b, rows : rows + 72, :] = jnp.zeros((72, 128), F32)
    lane = lax.broadcasted_iota(jnp.int32, (CELL, 384), 1)
    frame = 4 * lax.broadcasted_iota(jnp.int32, (CELL, 384), 0) + lane // 96

    def cell(c, _):
        b = start_ref[c]
        n = size_ref[c]
        row = b // 4
        phase = b - 4 * row
        now = jnp.concatenate([flat[i, pl.ds(row, CELL), :] for i in range(3)], axis=1)
        later = jnp.concatenate([flat[i, pl.ds(row + 1, CELL), :] for i in range(3)], axis=1)
        at = pl.multiple_of(c * CELL, CELL)
        for p in range(4):

            @pl.when(phase == p)
            def _():
                mixed = now if p == 0 else jnp.where(lane >= 96 * p, now, later)
                moved = mixed if p == 0 else jnp.concatenate([mixed[:, 96 * p :], mixed[:, : 96 * p]], axis=1)
                o_ref[pl.ds(at, CELL), :] = jnp.where(frame < n, moved, 0.0).astype(BF16)

        return 0

    lax.fori_loop(0, 32, cell, 0)


def attend_kernel(
    group_ref, lengths_ref, assignment_ref, q_ref, k_ref, v_ref, o_ref, qf, kf, vf, start_ref, size_ref, seen_ref
):
    cell_tables(group_ref[0], lengths_ref, assignment_ref, start_ref, size_ref, seen_ref)
    rows = q_ref.shape[0]

    def widen(i, _):
        r = pl.multiple_of(i * 128, 128)
        qf[pl.ds(r, 128), :] = q_ref[pl.ds(r, 128), :].astype(F32) * (HD**-0.5)
        kf[pl.ds(r, 128), :] = k_ref[pl.ds(r, 128), :].astype(F32)
        vf[pl.ds(r, 128), :] = v_ref[pl.ds(r, 128), :].astype(F32)
        return 0

    lax.fori_loop(0, rows // 128, widen, 0)
    for ref in (qf, kf, vf):
        ref[rows : rows + 136, :] = jnp.zeros((136, 128), F32)
    lane = lax.broadcasted_iota(jnp.int32, (CELL, 128), 1)
    low = lane < 64
    frame = 4 * lax.broadcasted_iota(jnp.int32, (CELL, 128), 0) + lane // 64
    lane2 = lax.broadcasted_iota(jnp.int32, (2 * CELL, 128), 1)
    low2 = lane2 < 64
    column = lax.broadcasted_iota(jnp.int32, (1, MAXLEN), 1)
    key_frame = 2 * (column % 128) + column // 128

    def doubled(ref, row, shift):
        now = ref[pl.ds(row, 2 * CELL), :]
        later = ref[pl.ds(row + 1, 2 * CELL), :]
        even = jnp.where(lane2 >= shift, now, later)
        other = pltpu.roll(even, 64, 1)
        swap = shift > 0
        first = jnp.where(low2, even, other)
        second = jnp.where(low2, other, even)
        return jnp.concatenate(
            [jnp.where(swap, second, first), jnp.where(swap, first, second)], axis=0
        ).astype(BF16)

    def cell(c):
        b = start_ref[c]
        n = size_ref[c]
        row = b // 2
        shift = 64 * (b - 2 * row)
        u0 = qf[pl.ds(row, CELL, stride=2), :]
        u1 = qf[pl.ds(row + 1, CELL, stride=2), :]
        u2 = qf[pl.ds(row + 2, CELL, stride=2), :]
        v0 = pltpu.roll(jnp.where(lane >= shift, u0, u1), shift, 1)
        v1 = pltpu.roll(jnp.where(lane >= shift, u1, u2), shift, 1)
        queries = jnp.concatenate(
            [
                jnp.where(low, v0, 0.0),
                jnp.where(low, 0.0, v0),
                jnp.where(low, v1, 0.0),
                jnp.where(low, 0.0, v1),
            ],
            axis=0,
        ).astype(BF16)
        keys = doubled(kf, row, shift)
        values = doubled(vf, row, shift)
        scores = lax.dot_general(queries, keys, NT, preferred_element_type=F32)
        scores = jnp.where(key_frame < n, scores, MASKED)
        exponentials = jnp.exp(scores - jnp.max(scores, axis=1, keepdims=True))
        total = jnp.sum(exponentials, axis=1, keepdims=True)
        weights = (exponentials / total).astype(BF16)
        context = jnp.dot(weights, values, preferred_element_type=F32)
        at = pl.multiple_of(c * CELL, CELL)
        first = jnp.where(low, context[0:64], context[64:128])
        second = jnp.where(low, context[128:192], context[192:256])
        o_ref[pl.ds(at, CELL), 0:128] = jnp.where(frame < n, first, 0.0).astype(BF16)
        o_ref[pl.ds(at, CELL), 128:256] = jnp.where(frame + 2 < n, second, 0.0).astype(BF16)

    def some(i, _):
        cell(2 * i)
        cell(2 * i + 1)
        return 0

    lax.fori_loop(0, 16, some, 0)


def compact_kernel(width, after_ref, x_ref, o_ref, flat):
    lanes = 4 * width
    blocks = lanes // 128
    total = flat.shape[1]
    slabs = o_ref.shape[0]

    def clear(i, _):
        r = pl.multiple_of(i * 16, 16)
        for b in range(blocks):
            flat[b, pl.ds(r, 16), :] = jnp.zeros((16, 128), F32)
        return 0

    lax.fori_loop(0, total // 16, clear, 0)
    lane = lax.broadcasted_iota(jnp.int32, (CELL, lanes), 1)

    def cell(c, _):
        first = after_ref[c]
        row = first // 4
        phase = first - 4 * row
        block = x_ref[pl.ds(pl.multiple_of(c * CELL, CELL), CELL), :].astype(F32)
        for p in range(4):

            @pl.when(phase == p)
            def _():
                s = p * width
                moved = block if p == 0 else jnp.concatenate([block[:, lanes - s :], block[:, : lanes - s]], axis=1)
                here = moved if p == 0 else jnp.where(lane >= s, moved, 0.0)
                for b in range(blocks):
                    at = (b, pl.ds(row + 8, CELL), slice(None))
                    flat[at] = flat[at] + here[:, 128 * b : 128 * b + 128]
                if p > 0:
                    below = jnp.where(lane >= s, 0.0, moved)
                    for b in range((s + 127) // 128):
                        at = (b, pl.ds(row + 9, CELL), slice(None))
                        flat[at] = flat[at] + below[:, 128 * b : 128 * b + 128]

        return 0

    lax.fori_loop(0, 32, cell, 0)

    def window(m, _):
        for b in range(blocks):
            o_ref[m, :, 128 * b : 128 * b + 128] = flat[b, pl.ds(pl.multiple_of(m * 128, 128), 144), :].astype(BF16)
        return 0

    lax.fori_loop(0, slabs, window, 0)


WIN = 144
EDGE = 8


def rest_kernel(
    slab_ref,
    ends_ref,
    x_ref,
    c_ref,
    w_ref,
    gain_ref,
    bias_ref,
    taps_ref,
    scale_ref,
    shift_ref,
    o_ref,
    wo,
    wg,
    wd,
    ctx,
    carried,
    normed,
    gated,
    segment,
    swished,
    turned,
    sems,
):
    slab = slab_ref[0]
    piece = 176

    def fetch(g, _):
        c = g // 16
        m = g - 16 * c
        base = pl.multiple_of(g * piece, 16)
        for s in range(3):
            pltpu.make_async_copy(
                w_ref.at[pl.ds(base, 32), pl.ds(512 * s, 512)],
                wo.at[pl.ds(pl.multiple_of(96 * m + 32 * s, 16), 32), pl.ds(pl.multiple_of(512 * c, 512), 512)],
                sems.at[0],
            ).start()
        return 0

    def fetch_glu(g, _):
        c = g // 16
        m = g - 16 * c
        base = pl.multiple_of(g * piece + 32, 16)
        pltpu.make_async_copy(
            w_ref.at[pl.ds(base, 96), :],
            wg.at[pl.ds(pl.multiple_of(192 * m + 96 * c, 16), 96), :],
            sems.at[1],
        ).start()
        return 0

    def fetch_down(g, _):
        c = g // 16
        m = g - 16 * c
        base = pl.multiple_of(g * piece + 128, 16)
        pltpu.make_async_copy(
            w_ref.at[pl.ds(base, 48), :],
            wd.at[pl.ds(pl.multiple_of(96 * m + 48 * c, 16), 48), :],
            sems.at[2],
        ).start()
        return 0

    lax.fori_loop(0, 32, fetch, 0)
    lax.fori_loop(0, 32, fetch_glu, 0)
    lax.fori_loop(0, 32, fetch_down, 0)

    for j in range(4):
        frame = 512 * slab - 4 * EDGE + j + 4 * lax.broadcasted_iota(jnp.int32, (WIN, 128), 0)

        def count(i, number):
            return number + jnp.where(frame >= ends_ref[i], 1, 0)

        number = lax.fori_loop(0, 32, count, jnp.where(frame >= 0, 0, -1))
        segment[j] = number.astype(F32)

    low = lax.broadcasted_iota(jnp.int32, (WIN, 128), 1) < 64

    def heads(h, _):
        at = pl.ds(pl.multiple_of(128 * h, 128), 128)
        for j in range(4):
            part = slice(128 * (j // 2), 128 * (j // 2) + 128)
            left = c_ref[2 * h, :, part].astype(F32)
            right = c_ref[2 * h + 1, :, part].astype(F32)
            if j % 2 == 0:
                right = pltpu.roll(right, 64, 1)
            else:
                left = pltpu.roll(left, 64, 1)
            ctx[WIN * j : WIN * j + WIN, at] = jnp.where(low, left, right).astype(BF16)
        return 0

    lax.fori_loop(0, 8, heads, 0)

    lane = lax.broadcasted_iota(jnp.int32, (WIN, 384), 1)

    def features(g, _):
        at = pl.ds(pl.multiple_of(384 * g, 128), 384)
        for j in range(4):
            whole = None
            for f in range(4):
                block = x_ref[4 * g + f].astype(F32)
                s = 96 * ((f - j) % 4)
                if s:
                    block = jnp.concatenate([block[:, 384 - s :], block[:, : 384 - s]], axis=1)
                if whole is None:
                    whole = block
                else:
                    whole = jnp.where(lane >= 96 * f, block, whole)
            carried[WIN * j : WIN * j + WIN, at] = whole
        return 0

    lax.fori_loop(0, 4, features, 0)

    pltpu.make_async_copy(wo, wo, sems.at[0]).wait()

    def project(n, _):
        at = pl.ds(pl.multiple_of(256 * n, 256), 256)
        carried[:, at] = carried[:, at] + lax.dot_general(
            ctx[...], wo[at, :], NT, preferred_element_type=F32
        )
        return 0

    lax.fori_loop(0, 6, project, 0)

    def norm(i, _):
        at = pl.ds(pl.multiple_of(32 * i, 32), 32)
        rows = carried[at, :]
        centred = rows - jnp.mean(rows, axis=1, keepdims=True)
        variance = jnp.mean(centred * centred, axis=1, keepdims=True)
        normed[at, :] = (centred * lax.rsqrt(variance + EPS) * gain_ref[...] + bias_ref[...]).astype(BF16)
        return 0

    lax.fori_loop(0, 4 * WIN // 32, norm, 0)

    pltpu.make_async_copy(wg, wg, sems.at[1]).wait()

    def glu(n, _):
        value = lax.dot_general(
            normed[...], wg[pl.ds(pl.multiple_of(256 * n, 256), 256), :], NT, preferred_element_type=F32
        )
        gate = lax.dot_general(
            normed[...], wg[pl.ds(pl.multiple_of(1536 + 256 * n, 256), 256), :], NT, preferred_element_type=F32
        )
        out = (value * jax.nn.sigmoid(gate)).astype(BF16).astype(F32)
        for j in range(4):
            for b in range(2):
                gated[2 * n + b, j] = out[WIN * j : WIN * j + WIN, 128 * b : 128 * b + 128]
        return 0

    lax.fori_loop(0, 6, glu, 0)

    def conv(b, _):
        at = pl.ds(pl.multiple_of(128 * b, 128), 128)
        taps = taps_ref[:, at]
        scale = scale_ref[:, at]
        shift = shift_ref[:, at]

        def chunk(i, _):
            row = EDGE + i * 8
            mine = [segment[j, pl.ds(pl.multiple_of(row, 8), 8), :] for j in range(4)]
            sums = [jnp.zeros((8, 128), F32) for _ in range(4)]
            for d in range(-4, 5):
                for p in range(4):
                    used = [j for j in range(4) if -HALF <= 4 * d + p - j <= HALF]
                    if not used:
                        continue
                    values = gated[b, p, pl.ds(row + d, 8), :]
                    owner = segment[p, pl.ds(row + d, 8), :]
                    for j in used:
                        t = 4 * d + p - j + HALF
                        sums[j] = sums[j] + jnp.where(owner == mine[j], values, 0.0) * taps[t : t + 1]
            for j in range(4):
                affine = sums[j] * scale + shift
                turned[0, pl.ds(pl.multiple_of(128 * j + 8 * i, 8), 8), :] = affine * jax.nn.sigmoid(affine)
            return 0

        lax.fori_loop(0, 16, chunk, 0)
        swished[:, at] = turned[0].astype(BF16)
        return 0

    lax.fori_loop(0, 12, conv, 0)

    pltpu.make_async_copy(wd, wd, sems.at[2]).wait()
    live = ends_ref[31]

    def down(n, _):
        at = pl.ds(pl.multiple_of(256 * n, 256), 256)
        lowered = lax.dot_general(swished[...], wd[at, :], NT, preferred_element_type=F32)
        for j in range(4):
            frame = 512 * slab + j + 4 * lax.broadcasted_iota(jnp.int32, (128, 256), 0)
            rows = carried[WIN * j + EDGE : WIN * j + EDGE + 128, at] + lowered[128 * j : 128 * j + 128]
            rows = jnp.where(frame < live, rows, 0.0)
            for b in range(2):
                turned[b, pl.ds(j, 128, stride=4), :] = rows[:, 128 * b : 128 * b + 128]
        o_ref[:, at] = jnp.concatenate([turned[0], turned[1]], axis=1).astype(BF16)
        return 0

    lax.fori_loop(0, 6, down, 0)


SMEM = pl.BlockSpec(memory_space=pltpu.SMEM)
VMEM = pl.BlockSpec(memory_space=pltpu.VMEM)
BIG = 60 * 1024 * 1024


def pack(group, lengths, assignment, x):
    rows = x.shape[0]
    return pl.pallas_call(
        pack_kernel,
        out_shape=jax.ShapeDtypeStruct((32 * CELL, 384), BF16),
        in_specs=[SMEM, SMEM, SMEM, VMEM],
        out_specs=VMEM,
        scratch_shapes=[
            pltpu.VMEM((3, rows + 72, 128), F32),
            pltpu.SMEM((32,), jnp.int32),
            pltpu.SMEM((32,), jnp.int32),
            pltpu.SMEM((8,), jnp.int32),
        ],
        compiler_params=pltpu.CompilerParams(vmem_limit_bytes=24 * 1024 * 1024),
        cost_estimate=pl.CostEstimate(flops=20_000_000, bytes_accessed=3_200_000, transcendentals=0),
        name="pack_cells",
    )(group, lengths, assignment, x)


def attend(group, lengths, assignment, q, k, v):
    rows = q.shape[0]
    return pl.pallas_call(
        attend_kernel,
        out_shape=jax.ShapeDtypeStruct((32 * CELL, 256), BF16),
        in_specs=[SMEM, SMEM, SMEM, VMEM, VMEM, VMEM],
        out_specs=VMEM,
        scratch_shapes=[
            pltpu.VMEM((rows + 136, 128), F32),
            pltpu.VMEM((rows + 136, 128), F32),
            pltpu.VMEM((rows + 136, 128), F32),
            pltpu.SMEM((32,), jnp.int32),
            pltpu.SMEM((32,), jnp.int32),
            pltpu.SMEM((8,), jnp.int32),
        ],
        compiler_params=pltpu.CompilerParams(vmem_limit_bytes=32 * 1024 * 1024),
        cost_estimate=pl.CostEstimate(flops=2_000_000_000, bytes_accessed=4_200_000, transcendentals=2_000_000),
        name="attend_cells",
    )(group, lengths, assignment, q, k, v)


def compact(width, after, cells, slabs):
    lanes = 4 * width
    return pl.pallas_call(
        functools.partial(compact_kernel, width),
        out_shape=jax.ShapeDtypeStruct((slabs, WIN, lanes), BF16),
        in_specs=[SMEM, VMEM],
        out_specs=VMEM,
        scratch_shapes=[pltpu.VMEM((lanes // 128, 32 * CELL + 80, 128), F32)],
        compiler_params=pltpu.CompilerParams(vmem_limit_bytes=24 * 1024 * 1024),
        cost_estimate=pl.CostEstimate(flops=20_000_000, bytes_accessed=3_200_000, transcendentals=0),
        name="compact_cells",
    )(after, cells)


def rest(slab, ends, x, c, w, gain, bias, taps, scale, shift):
    return pl.pallas_call(
        rest_kernel,
        out_shape=jax.ShapeDtypeStruct((512, 1536), BF16),
        in_specs=[SMEM, SMEM, VMEM, VMEM, pl.BlockSpec(memory_space=pl.ANY)] + [VMEM] * 5,
        out_specs=VMEM,
        scratch_shapes=[
            pltpu.VMEM((1536, 1024), BF16),
            pltpu.VMEM((3072, 1536), BF16),
            pltpu.VMEM((1536, 1536), BF16),
            pltpu.VMEM((4 * WIN, 1024), BF16),
            pltpu.VMEM((4 * WIN, 1536), F32),
            pltpu.VMEM((4 * WIN, 1536), BF16),
            pltpu.VMEM((12, 4, WIN, 128), F32),
            pltpu.VMEM((4, WIN, 128), F32),
            pltpu.VMEM((512, 1536), BF16),
            pltpu.VMEM((2, 512, 128), F32),
            pltpu.SemaphoreType.DMA((3,)),
        ],
        compiler_params=pltpu.CompilerParams(vmem_limit_bytes=BIG),
        cost_estimate=pl.CostEstimate(flops=9_000_000_000, bytes_accessed=25_000_000, transcendentals=2_000_000),
        name="project_and_convolve",
    )(slab, ends, x, c, w, gain, bias, taps, scale, shift)


def target_tables(data_group, lengths, assignment):
    count = lengths.shape[0]
    number = jnp.arange(count, dtype=jnp.int32)
    mine = assignment == data_group
    place = jnp.sum(jnp.where((number[None, :] < number[:, None]) & mine[None, :], 1, 0), axis=1)
    slot = jnp.arange(32, dtype=jnp.int32)
    spans = jnp.sum(jnp.where(mine[None, :] & (place[None, :] == slot[:, None]), lengths[None, :], 0), axis=1)
    first = jnp.sum(jnp.where(slot[None, :] < slot[:, None], spans[None, :], 0), axis=1)
    return first, first + spans


def on_device(
    query_rows,
    key_rows,
    value_rows,
    residual,
    lengths,
    assignment,
    out_proj,
    norm_gain,
    norm_bias,
    glu_proj,
    conv_taps,
    batch_scale,
    batch_shift,
    down_proj,
):
    data_group = lax.axis_index("dp").astype(jnp.int32)
    slab = lax.axis_index("mp").astype(jnp.int32)
    groups = lax.axis_size("dp")
    slabs = lax.axis_size("mp")
    core = data_group % 2
    op = lax.dynamic_slice_in_dim(out_proj.T, core * 512, 512, 1)
    op = jnp.concatenate([op[0:32], op[32:64], op[64:96]], axis=1)
    glu = lax.dynamic_slice_in_dim(glu_proj.T, core * 96, 96, 0)
    dn = lax.dynamic_slice_in_dim(down_proj.T, core * 48, 48, 0)
    mine = jnp.concatenate([op, glu, dn], axis=0)
    chips = [[(2 * p + c) * slabs + m for c in range(2) for m in range(slabs)] for p in range(groups // 2)]
    weights = lax.all_gather(mine, ("dp", "mp"), axis=0, tiled=True, axis_index_groups=chips)

    group = data_group.reshape(1)
    x_cells = pack(group, lengths, assignment, residual.reshape(residual.shape[0], 384))
    x_here = lax.all_to_all(
        x_cells.reshape(groups, 4 * CELL, 384), "dp", split_axis=0, concat_axis=0, tiled=True
    )
    c_cells = attend(
        group,
        lengths,
        assignment,
        query_rows.reshape(-1, 128),
        key_rows.reshape(-1, 128),
        value_rows.reshape(-1, 128),
    )
    c_here = lax.all_to_all(
        c_cells.reshape(groups, 4 * CELL, 256), "dp", split_axis=0, concat_axis=0, tiled=True
    )
    first, ends = target_tables(data_group, lengths, assignment)
    x_slab = lax.all_to_all(
        compact(96, first, x_here.reshape(-1, 384), slabs), "mp", split_axis=0, concat_axis=0, tiled=True
    )
    c_slab = lax.all_to_all(
        compact(64, first, c_here.reshape(-1, 256), slabs), "mp", split_axis=0, concat_axis=0, tiled=True
    )
    row = lambda a: a.reshape(1, -1)
    return rest(
        slab.reshape(1),
        ends,
        x_slab,
        c_slab,
        weights,
        row(norm_gain),
        row(norm_bias),
        conv_taps,
        row(batch_scale),
        row(batch_shift),
    )


def solution(mesh):
    in_specs = (
        P("dp", "mp", None),
        P("dp", "mp", None),
        P("dp", "mp", None),
        P("dp", "mp", None),
        P(),
        P(),
        P(None, "mp"),
        P(),
        P(),
        P(None, "mp"),
        P(),
        P(),
        P(),
        P(None, "mp"),
    )
    out_specs = P(("dp", "mp"), None)
    return jax.shard_map(
        on_device, mesh=mesh, in_specs=in_specs, out_specs=out_specs, check_vma=False
    )
```

```python
import functools

import jax
import jax.numpy as jnp
from jax import lax
from jax.experimental import pallas as pl
from jax.experimental.pallas import tpu as pltpu
from jax.sharding import PartitionSpec as P

HD = 64
KERNEL = 31
HALF = 15
MAXLEN = 256
EPS = 1e-05
MASKED = -1e30

CELL = MAXLEN // 4
F32 = jnp.float32
BF16 = jnp.bfloat16
NT = (((1,), (1,)), ((), ()))


def cell_tables(data_group, lengths_ref, assignment_ref, start_ref, size_ref, seen_ref):
    per_group = 32
    for t in range(8):
        seen_ref[t] = 0

    def step(i, at):
        u = data_group * per_group + i
        t = assignment_ref[u]
        n = lengths_ref[u]
        k = seen_ref[t]
        seen_ref[t] = k + 1
        start_ref[4 * t + k] = at
        size_ref[4 * t + k] = n
        return at + n

    lax.fori_loop(0, per_group, step, jnp.int32(0))


def pack_kernel(group_ref, lengths_ref, assignment_ref, x_ref, o_ref, flat, start_ref, size_ref, seen_ref):
    cell_tables(group_ref[0], lengths_ref, assignment_ref, start_ref, size_ref, seen_ref)
    rows = x_ref.shape[0]

    def widen(i, _):
        r = pl.multiple_of(i * 64, 64)
        for b in range(3):
            flat[b, pl.ds(r, 64), :] = x_ref[pl.ds(r, 64), 128 * b : 128 * b + 128].astype(F32)
        return 0

    lax.fori_loop(0, rows // 64, widen, 0)
    for b in range(3):
        flat[b, rows : rows + 72, :] = jnp.zeros((72, 128), F32)
    lane = lax.broadcasted_iota(jnp.int32, (CELL, 384), 1)
    frame = 4 * lax.broadcasted_iota(jnp.int32, (CELL, 384), 0) + lane // 96

    def cell(c, _):
        b = start_ref[c]
        n = size_ref[c]
        row = b // 4
        phase = b - 4 * row
        now = jnp.concatenate([flat[i, pl.ds(row, CELL), :] for i in range(3)], axis=1)
        later = jnp.concatenate([flat[i, pl.ds(row + 1, CELL), :] for i in range(3)], axis=1)
        at = pl.multiple_of(c * CELL, CELL)
        for p in range(4):

            @pl.when(phase == p)
            def _():
                mixed = now if p == 0 else jnp.where(lane >= 96 * p, now, later)
                moved = mixed if p == 0 else jnp.concatenate([mixed[:, 96 * p :], mixed[:, : 96 * p]], axis=1)
                o_ref[pl.ds(at, CELL), :] = jnp.where(frame < n, moved, 0.0).astype(BF16)

        return 0

    lax.fori_loop(0, 32, cell, 0)


def attend_kernel(
    group_ref, lengths_ref, assignment_ref, q_ref, k_ref, v_ref, *rest
):
    outs, (qf, kf, vf, o_ref, start_ref, size_ref, seen_ref) = rest[:8], rest[8:]
    cell_tables(group_ref[0], lengths_ref, assignment_ref, start_ref, size_ref, seen_ref)
    rows = q_ref.shape[0]

    def widen(i, _):
        r = pl.multiple_of(i * 128, 128)
        qf[pl.ds(r, 128), :] = q_ref[pl.ds(r, 128), :].astype(F32) * (HD**-0.5)
        kf[pl.ds(r, 128), :] = k_ref[pl.ds(r, 128), :].astype(F32)
        vf[pl.ds(r, 128), :] = v_ref[pl.ds(r, 128), :].astype(F32)
        return 0

    lax.fori_loop(0, rows // 128, widen, 0)
    for ref in (qf, kf, vf):
        ref[rows : rows + 136, :] = jnp.zeros((136, 128), F32)
    lane = lax.broadcasted_iota(jnp.int32, (CELL, 128), 1)
    low = lane < 64
    frame = 4 * lax.broadcasted_iota(jnp.int32, (CELL, 128), 0) + lane // 64
    lane2 = lax.broadcasted_iota(jnp.int32, (2 * CELL, 128), 1)
    low2 = lane2 < 64
    column = lax.broadcasted_iota(jnp.int32, (1, MAXLEN), 1)
    key_frame = 2 * (column % 128) + column // 128

    def doubled(ref, row, shift):
        now = ref[pl.ds(row, 2 * CELL), :]
        later = ref[pl.ds(row + 1, 2 * CELL), :]
        even = jnp.where(lane2 >= shift, now, later)
        other = pltpu.roll(even, 64, 1)
        swap = shift > 0
        first = jnp.where(low2, even, other)
        second = jnp.where(low2, other, even)
        return jnp.concatenate(
            [jnp.where(swap, second, first), jnp.where(swap, first, second)], axis=0
        ).astype(BF16)

    def cell(c):
        b = start_ref[c]
        n = size_ref[c]
        row = b // 2
        shift = 64 * (b - 2 * row)
        u0 = qf[pl.ds(row, CELL, stride=2), :]
        u1 = qf[pl.ds(row + 1, CELL, stride=2), :]
        u2 = qf[pl.ds(row + 2, CELL, stride=2), :]
        v0 = pltpu.roll(jnp.where(lane >= shift, u0, u1), shift, 1)
        v1 = pltpu.roll(jnp.where(lane >= shift, u1, u2), shift, 1)
        queries = jnp.concatenate(
            [
                jnp.where(low, v0, 0.0),
                jnp.where(low, 0.0, v0),
                jnp.where(low, v1, 0.0),
                jnp.where(low, 0.0, v1),
            ],
            axis=0,
        ).astype(BF16)
        keys = doubled(kf, row, shift)
        values = doubled(vf, row, shift)
        scores = lax.dot_general(queries, keys, NT, preferred_element_type=F32)
        scores = jnp.where(key_frame < n, scores, MASKED)
        exponentials = jnp.exp(scores - jnp.max(scores, axis=1, keepdims=True))
        total = jnp.sum(exponentials, axis=1, keepdims=True)
        weights = (exponentials / total).astype(BF16)
        context = jnp.dot(weights, values, preferred_element_type=F32)
        at = pl.multiple_of(c * CELL, CELL)
        first = jnp.where(low, context[0:64], context[64:128])
        second = jnp.where(low, context[128:192], context[192:256])
        o_ref[pl.ds(at, CELL), 0:128] = jnp.where(frame < n, first, 0.0).astype(BF16)
        o_ref[pl.ds(at, CELL), 128:256] = jnp.where(frame + 2 < n, second, 0.0).astype(BF16)

    def some(i, _):
        cell(2 * i)
        cell(2 * i + 1)
        return 0

    lax.fori_loop(0, 16, some, 0)
    for s in range(8):
        at = pl.multiple_of((group_ref[0] ^ s) * 4 * CELL, 4 * CELL)
        outs[s][...] = o_ref[pl.ds(at, 4 * CELL), :]


def compact_kernel(width, group_ref, after_ref, *rest):
    parts, (o_ref, flat) = rest[:-2], rest[-2:]
    lanes = 4 * width
    blocks = lanes // 128
    total = flat.shape[1]
    slabs = o_ref.shape[0]

    def clear(i, _):
        r = pl.multiple_of(i * 16, 16)
        for b in range(blocks):
            flat[b, pl.ds(r, 16), :] = jnp.zeros((16, 128), F32)
        return 0

    lax.fori_loop(0, total // 16, clear, 0)
    lane = lax.broadcasted_iota(jnp.int32, (CELL, lanes), 1)

    def cell(x_ref, from_group, k):
        first = after_ref[4 * from_group + k]
        row = first // 4
        phase = first - 4 * row
        block = x_ref[pl.ds(pl.multiple_of(k * CELL, CELL), CELL), :].astype(F32)
        for p in range(4):

            @pl.when(phase == p)
            def _():
                s = p * width
                moved = block if p == 0 else jnp.concatenate([block[:, lanes - s :], block[:, : lanes - s]], axis=1)
                here = moved if p == 0 else jnp.where(lane >= s, moved, 0.0)
                for b in range(blocks):
                    at = (b, pl.ds(row + 8, CELL), slice(None))
                    flat[at] = flat[at] + here[:, 128 * b : 128 * b + 128]
                if p > 0:
                    below = jnp.where(lane >= s, 0.0, moved)
                    for b in range((s + 127) // 128):
                        at = (b, pl.ds(row + 9, CELL), slice(None))
                        flat[at] = flat[at] + below[:, 128 * b : 128 * b + 128]

    if len(parts) == 1:

        def whole(c, _):
            cell(parts[0], 0, c)
            return 0

        lax.fori_loop(0, 32, whole, 0)
    else:
        for s, part in enumerate(parts):

            def some(k, _):
                cell(part, group_ref[0] ^ s, k)
                return 0

            lax.fori_loop(0, 4, some, 0)

    def window(m, _):
        for b in range(blocks):
            o_ref[m, :, 128 * b : 128 * b + 128] = flat[b, pl.ds(pl.multiple_of(m * 128, 128), 144), :].astype(BF16)
        return 0

    lax.fori_loop(0, slabs, window, 0)


WIN = 144
EDGE = 8


def widen_kernel(slab_ref, ends_ref, x_ref, o_ref, segment_ref):
    slab = slab_ref[0]
    lane = lax.broadcasted_iota(jnp.int32, (WIN, 384), 1)

    def features(g, _):
        at = pl.ds(pl.multiple_of(384 * g, 128), 384)
        blocks = [x_ref[4 * g + f].astype(F32) for f in range(4)]
        for j in range(4):
            whole = None
            for f in range(4):
                s = 96 * ((f - j) % 4)
                block = blocks[f]
                if s:
                    block = jnp.concatenate([block[:, 384 - s :], block[:, : 384 - s]], axis=1)
                whole = block if whole is None else jnp.where(lane >= 96 * f, block, whole)
            o_ref[WIN * j : WIN * j + WIN, at] = whole.astype(BF16)
        return 0

    lax.fori_loop(0, 4, features, 0)
    for j in range(4):
        frame = 512 * slab - 4 * EDGE + j + 4 * lax.broadcasted_iota(jnp.int32, (WIN, 128), 0)

        def count(i, number):
            return number + jnp.where(frame >= ends_ref[i], 1, 0)

        number = lax.fori_loop(0, 32, count, jnp.where(frame >= 0, 0, -1))
        segment_ref[j] = number.astype(F32)


def rest_kernel(
    slab_ref,
    ends_ref,
    x_ref,
    segment,
    c_ref,
    w_ref,
    gain_ref,
    bias_ref,
    taps_ref,
    scale_ref,
    shift_ref,
    o_ref,
    wo,
    wg,
    wd,
    ctx,
    carried,
    normed,
    gated,
    sums,
    swished,
    turned,
    sems,
):
    slab = slab_ref[0]
    piece = 176

    def fetch(g, _):
        c = g // 16
        m = g - 16 * c
        base = pl.multiple_of(g * piece, 16)
        for s in range(3):
            pltpu.make_async_copy(
                w_ref.at[pl.ds(base, 32), pl.ds(512 * s, 512)],
                wo.at[pl.ds(pl.multiple_of(96 * m + 32 * s, 16), 32), pl.ds(pl.multiple_of(512 * c, 512), 512)],
                sems.at[0],
            ).start()
        return 0

    def fetch_glu(g, _):
        c = g // 16
        m = g - 16 * c
        base = pl.multiple_of(g * piece + 32, 16)
        pltpu.make_async_copy(
            w_ref.at[pl.ds(base, 96), :],
            wg.at[pl.ds(pl.multiple_of(192 * m + 96 * c, 16), 96), :],
            sems.at[1],
        ).start()
        return 0

    def fetch_down(g, _):
        c = g // 16
        m = g - 16 * c
        base = pl.multiple_of(g * piece + 128, 16)
        pltpu.make_async_copy(
            w_ref.at[pl.ds(base, 48), :],
            wd.at[pl.ds(pl.multiple_of(96 * m + 48 * c, 16), 48), :],
            sems.at[2],
        ).start()
        return 0

    lax.fori_loop(0, 32, fetch, 0)
    lax.fori_loop(0, 32, fetch_glu, 0)
    lax.fori_loop(0, 32, fetch_down, 0)

    low = lax.broadcasted_iota(jnp.int32, (WIN, 128), 1) < 64

    def heads(h, _):
        at = pl.ds(pl.multiple_of(128 * h, 128), 128)
        for j in range(4):
            part = slice(128 * (j // 2), 128 * (j // 2) + 128)
            left = c_ref[2 * h, :, part].astype(F32)
            right = c_ref[2 * h + 1, :, part].astype(F32)
            if j % 2 == 0:
                right = pltpu.roll(right, 64, 1)
            else:
                left = pltpu.roll(left, 64, 1)
            ctx[WIN * j : WIN * j + WIN, at] = jnp.where(low, left, right).astype(BF16)
        return 0

    lax.fori_loop(0, 8, heads, 0)

    pltpu.make_async_copy(wo, wo, sems.at[0]).wait()

    def project(n, _):
        at = pl.ds(pl.multiple_of(256 * n, 256), 256)
        carried[:, at] = x_ref[:, at].astype(F32) + lax.dot_general(
            ctx[...], wo[at, :], NT, preferred_element_type=F32
        )
        return 0

    lax.fori_loop(0, 6, project, 0)

    def norm(i, _):
        at = pl.ds(pl.multiple_of(16 * i, 16), 16)
        rows = carried[at, :]
        centred = rows - jnp.mean(rows, axis=1, keepdims=True)
        variance = jnp.mean(centred * centred, axis=1, keepdims=True)
        normed[at, :] = (centred * lax.rsqrt(variance + EPS) * gain_ref[...] + bias_ref[...]).astype(BF16)
        return 0

    lax.fori_loop(0, 4 * WIN // 16, norm, 0, unroll=4)

    pltpu.make_async_copy(wg, wg, sems.at[1]).wait()

    def glu(n, _):
        value = lax.dot_general(
            normed[...], wg[pl.ds(pl.multiple_of(256 * n, 256), 256), :], NT, preferred_element_type=F32
        )
        gate = lax.dot_general(
            normed[...], wg[pl.ds(pl.multiple_of(1536 + 256 * n, 256), 256), :], NT, preferred_element_type=F32
        )
        out = (value * jax.nn.sigmoid(gate)).astype(BF16).astype(F32)
        for j in range(4):
            for b in range(2):
                gated[2 * n + b, j] = out[WIN * j : WIN * j + WIN, 128 * b : 128 * b + 128]
        return 0

    lax.fori_loop(0, 6, glu, 0)

    def conv(b, _):
        lanes = [pl.ds(pl.multiple_of(512 * b + 128 * l, 128), 128) for l in range(4)]
        for first, last in ((-15, -8), (-7, 0), (1, 8), (9, 15)):
            taps = [
                {o: jnp.broadcast_to(taps_ref[o + HALF : o + HALF + 1, at], (8, 128)) for o in range(first, last + 1)}
                for at in lanes
            ]

            def chunk(i, _):
                row = EDGE + i * 8
                for pair in ((0, 1), (2, 3)):
                    mine = {j: segment[j, pl.ds(pl.multiple_of(row, 8), 8), :] for j in pair}
                    rows = {j: pl.ds(pl.multiple_of(128 * j + 8 * i, 8), 8) for j in pair}
                    total = {(l, j): None if first == -15 else sums[l, rows[j], :] for l in range(4) for j in pair}
                    for e in range(first + pair[0], last + pair[1] + 1):
                        d, p = e // 4, e % 4
                        values = [gated[4 * b + l, p, pl.ds(row + d, 8), :] for l in range(4)]
                        owner = segment[p, pl.ds(row + d, 8), :]
                        for j in pair:
                            if not first <= e - j <= last:
                                continue
                            same = owner == mine[j]
                            for l in range(4):
                                term = jnp.where(same, values[l], 0.0) * taps[l][e - j]
                                total[l, j] = term if total[l, j] is None else total[l, j] + term
                    for j in pair:
                        for l in range(4):
                            sums[l, rows[j], :] = total[l, j]
                return 0

            lax.fori_loop(0, 16, chunk, 0)
        for l, at in enumerate(lanes):
            affine = sums[l] * scale_ref[:, at] + shift_ref[:, at]
            swished[:, at] = (affine * jax.nn.sigmoid(affine)).astype(BF16)
        return 0

    lax.fori_loop(0, 3, conv, 0)

    pltpu.make_async_copy(wd, wd, sems.at[2]).wait()
    live = ends_ref[31]

    def down(n, _):
        at = pl.ds(pl.multiple_of(256 * n, 256), 256)
        lowered = lax.dot_general(swished[...], wd[at, :], NT, preferred_element_type=F32)
        for j in range(4):
            frame = 512 * slab + j + 4 * lax.broadcasted_iota(jnp.int32, (128, 256), 0)
            rows = carried[WIN * j + EDGE : WIN * j + EDGE + 128, at] + lowered[128 * j : 128 * j + 128]
            rows = jnp.where(frame < live, rows, 0.0)
            for b in range(2):
                turned[b, pl.ds(j, 128, stride=4), :] = rows[:, 128 * b : 128 * b + 128]
        o_ref[:, at] = jnp.concatenate([turned[0], turned[1]], axis=1).astype(BF16)
        return 0

    lax.fori_loop(0, 6, down, 0)


SMEM = pl.BlockSpec(memory_space=pltpu.SMEM)
VMEM = pl.BlockSpec(memory_space=pltpu.VMEM)
BIG = 60 * 1024 * 1024


def pack(group, lengths, assignment, x):
    rows = x.shape[0]
    return pl.pallas_call(
        pack_kernel,
        out_shape=jax.ShapeDtypeStruct((32 * CELL, 384), BF16),
        in_specs=[SMEM, SMEM, SMEM, VMEM],
        out_specs=VMEM,
        scratch_shapes=[
            pltpu.VMEM((3, rows + 72, 128), F32),
            pltpu.SMEM((32,), jnp.int32),
            pltpu.SMEM((32,), jnp.int32),
            pltpu.SMEM((8,), jnp.int32),
        ],
        compiler_params=pltpu.CompilerParams(vmem_limit_bytes=24 * 1024 * 1024),
        cost_estimate=pl.CostEstimate(flops=20_000_000, bytes_accessed=3_200_000, transcendentals=0),
        name="pack_cells",
    )(group, lengths, assignment, x)


def attend(group, lengths, assignment, q, k, v):
    rows = q.shape[0]
    return pl.pallas_call(
        attend_kernel,
        out_shape=[jax.ShapeDtypeStruct((4 * CELL, 256), BF16)] * 8,
        in_specs=[SMEM, SMEM, SMEM, VMEM, VMEM, VMEM],
        out_specs=[VMEM] * 8,
        scratch_shapes=[
            pltpu.VMEM((rows + 136, 128), F32),
            pltpu.VMEM((rows + 136, 128), F32),
            pltpu.VMEM((rows + 136, 128), F32),
            pltpu.VMEM((32 * CELL, 256), BF16),
            pltpu.SMEM((32,), jnp.int32),
            pltpu.SMEM((32,), jnp.int32),
            pltpu.SMEM((8,), jnp.int32),
        ],
        compiler_params=pltpu.CompilerParams(vmem_limit_bytes=32 * 1024 * 1024),
        cost_estimate=pl.CostEstimate(flops=2_000_000_000, bytes_accessed=4_200_000, transcendentals=2_000_000),
        name="attend_cells",
    )(group, lengths, assignment, q, k, v)


def compact(width, group, after, cells, slabs):
    lanes = 4 * width
    return pl.pallas_call(
        functools.partial(compact_kernel, width),
        out_shape=jax.ShapeDtypeStruct((slabs, WIN, lanes), BF16),
        in_specs=[SMEM, SMEM] + [VMEM] * len(cells),
        out_specs=VMEM,
        scratch_shapes=[pltpu.VMEM((lanes // 128, 32 * CELL + 80, 128), F32)],
        compiler_params=pltpu.CompilerParams(vmem_limit_bytes=24 * 1024 * 1024),
        cost_estimate=pl.CostEstimate(flops=20_000_000, bytes_accessed=3_200_000, transcendentals=0),
        name="compact_cells",
    )(group, after, *cells)


def widen(slab, ends, x):
    return pl.pallas_call(
        widen_kernel,
        out_shape=[jax.ShapeDtypeStruct((4 * WIN, 1536), BF16), jax.ShapeDtypeStruct((4, WIN, 128), F32)],
        in_specs=[SMEM, SMEM, VMEM],
        out_specs=[VMEM, VMEM],
        compiler_params=pltpu.CompilerParams(vmem_limit_bytes=24 * 1024 * 1024),
        cost_estimate=pl.CostEstimate(flops=20_000_000, bytes_accessed=4_000_000, transcendentals=0),
        name="side_by_side",
    )(slab, ends, x)


def rest(slab, ends, x, segment, c, w, gain, bias, taps, scale, shift):
    return pl.pallas_call(
        rest_kernel,
        out_shape=jax.ShapeDtypeStruct((512, 1536), BF16),
        in_specs=[SMEM, SMEM, VMEM, VMEM, VMEM, pl.BlockSpec(memory_space=pl.ANY)] + [VMEM] * 5,
        out_specs=VMEM,
        scratch_shapes=[
            pltpu.VMEM((1536, 1024), BF16),
            pltpu.VMEM((3072, 1536), BF16),
            pltpu.VMEM((1536, 1536), BF16),
            pltpu.VMEM((4 * WIN, 1024), BF16),
            pltpu.VMEM((4 * WIN, 1536), F32),
            pltpu.VMEM((4 * WIN, 1536), BF16),
            pltpu.VMEM((12, 4, WIN, 128), F32),
            pltpu.VMEM((4, 512, 128), F32),
            pltpu.VMEM((512, 1536), BF16),
            pltpu.VMEM((2, 512, 128), F32),
            pltpu.SemaphoreType.DMA((3,)),
        ],
        compiler_params=pltpu.CompilerParams(vmem_limit_bytes=BIG),
        cost_estimate=pl.CostEstimate(flops=9_000_000_000, bytes_accessed=25_000_000, transcendentals=2_000_000),
        name="project_and_convolve",
    )(slab, ends, x, segment, c, w, gain, bias, taps, scale, shift)


def target_tables(data_group, lengths, assignment):
    count = lengths.shape[0]
    number = jnp.arange(count, dtype=jnp.int32)
    mine = assignment == data_group
    place = jnp.sum(jnp.where((number[None, :] < number[:, None]) & mine[None, :], 1, 0), axis=1)
    slot = jnp.arange(32, dtype=jnp.int32)
    spans = jnp.sum(jnp.where(mine[None, :] & (place[None, :] == slot[:, None]), lengths[None, :], 0), axis=1)
    first = jnp.sum(jnp.where(slot[None, :] < slot[:, None], spans[None, :], 0), axis=1)
    return first, first + spans


def on_device(
    query_rows,
    key_rows,
    value_rows,
    residual,
    lengths,
    assignment,
    out_proj,
    norm_gain,
    norm_bias,
    glu_proj,
    conv_taps,
    batch_scale,
    batch_shift,
    down_proj,
):
    data_group = lax.axis_index("dp").astype(jnp.int32)
    slab = lax.axis_index("mp").astype(jnp.int32)
    groups = lax.axis_size("dp")
    slabs = lax.axis_size("mp")
    core = data_group % 2
    op = lax.dynamic_slice_in_dim(out_proj.T, core * 512, 512, 1)
    op = jnp.concatenate([op[0:32], op[32:64], op[64:96]], axis=1)
    glu = lax.dynamic_slice_in_dim(glu_proj.T, core * 96, 96, 0)
    dn = lax.dynamic_slice_in_dim(down_proj.T, core * 48, 48, 0)
    mine = jnp.concatenate([op, glu, dn], axis=0)
    chips = [[(2 * p + c) * slabs + m for c in range(2) for m in range(slabs)] for p in range(groups // 2)]
    weights = lax.all_gather(mine, ("dp", "mp"), axis=0, tiled=True, axis_index_groups=chips)

    group = data_group.reshape(1)
    x_cells = pack(group, lengths, assignment, residual.reshape(residual.shape[0], 384))
    x_here = lax.all_to_all(
        x_cells.reshape(groups, 4 * CELL, 384), "dp", split_axis=0, concat_axis=0, tiled=True
    )
    group_later, _ = lax.optimization_barrier((group, x_cells))
    c_cells = attend(
        group_later,
        lengths,
        assignment,
        query_rows.reshape(-1, 128),
        key_rows.reshape(-1, 128),
        value_rows.reshape(-1, 128),
    )
    x_here, first_cells = lax.optimization_barrier((x_here, c_cells[0]))
    c_here = [first_cells] + [
        lax.ppermute(c_cells[s], "dp", [(i, i ^ s) for i in range(groups)]) for s in range(1, groups)
    ]
    first, ends = target_tables(data_group, lengths, assignment)
    x_slab = lax.all_to_all(
        compact(96, group, first, [x_here.reshape(-1, 384)], slabs), "mp", split_axis=0, concat_axis=0, tiled=True
    )
    c_slab = lax.all_to_all(
        compact(64, group, first, c_here, slabs), "mp", split_axis=0, concat_axis=0, tiled=True
    )
    slab = slab.reshape(1)
    x_wide, segment = widen(slab, ends, x_slab)
    row = lambda a: a.reshape(1, -1)
    return rest(
        slab,
        ends,
        x_wide,
        segment,
        c_slab,
        weights,
        row(norm_gain),
        row(norm_bias),
        conv_taps,
        row(batch_scale),
        row(batch_shift),
    )


def solution(mesh):
    in_specs = (
        P("dp", "mp", None),
        P("dp", "mp", None),
        P("dp", "mp", None),
        P("dp", "mp", None),
        P(),
        P(),
        P(None, "mp"),
        P(),
        P(),
        P(None, "mp"),
        P(),
        P(),
        P(),
        P(None, "mp"),
    )
    out_specs = P(("dp", "mp"), None)
    return jax.shard_map(
        on_device, mesh=mesh, in_specs=in_specs, out_specs=out_specs, check_vma=False
    )
```

```python
import functools

import jax
import jax.numpy as jnp
from jax import lax
from jax.experimental import pallas as pl
from jax.experimental.pallas import tpu as pltpu
from jax.sharding import PartitionSpec as P

HD = 64
KERNEL = 31
HALF = 15
MAXLEN = 256
EPS = 1e-05
MASKED = -1e30

CELL = MAXLEN // 4
F32 = jnp.float32
BF16 = jnp.bfloat16
NT = (((1,), (1,)), ((), ()))


def cell_tables(data_group, lengths_ref, assignment_ref, start_ref, size_ref, seen_ref):
    per_group = 32
    for t in range(8):
        seen_ref[t] = 0

    def step(i, at):
        u = data_group * per_group + i
        t = assignment_ref[u]
        n = lengths_ref[u]
        k = seen_ref[t]
        seen_ref[t] = k + 1
        start_ref[4 * t + k] = at
        size_ref[4 * t + k] = n
        return at + n

    lax.fori_loop(0, per_group, step, jnp.int32(0))


def turn(x, s):
    return jnp.concatenate([x[:, s:], x[:, :s]], axis=1)


def pack_kernel(
    group_ref, lengths_ref, assignment_ref, x_ref, o_ref, flat, packed, start_ref, size_ref, seen_ref, sem
):
    cell_tables(group_ref[0], lengths_ref, assignment_ref, start_ref, size_ref, seen_ref)
    rows = x_ref.shape[0]

    def widen(i, _):
        r = pl.multiple_of(i * 64, 64)
        for b in range(3):
            flat[b, pl.ds(r, 64), :] = x_ref[pl.ds(r, 64), 128 * b : 128 * b + 128].astype(F32)
        return 0

    lax.fori_loop(0, rows // 64, widen, 0)
    for b in range(3):
        flat[b, rows : rows + 72, :] = jnp.zeros((72, 128), F32)
    lane = lax.broadcasted_iota(jnp.int32, (CELL, 384), 1)
    frame = 4 * lax.broadcasted_iota(jnp.int32, (CELL, 384), 0) + lane // 96

    def cell(c):
        b = start_ref[c]
        row = b // 4
        phase = b - 4 * row
        now = jnp.concatenate([flat[i, pl.ds(row, CELL), :] for i in range(3)], axis=1)
        later = jnp.concatenate([flat[i, pl.ds(row + 1, CELL), :] for i in range(3)], axis=1)
        mixed = jnp.where(lane >= 96 * phase, now, later)
        mixed = jnp.where(phase >= 2, turn(mixed, 192), mixed)
        mixed = jnp.where(phase % 2 == 1, turn(mixed, 96), mixed)
        return jnp.where(frame < size_ref[c], mixed, 0.0).astype(BF16)

    def target(t, _):
        parts = [cell(4 * t + k) for k in range(4)]
        at = pl.multiple_of(4 * CELL * t, 4 * CELL)
        for k, part in enumerate(parts):
            packed[pl.ds(at + k * CELL, CELL), :] = part
        pltpu.make_async_copy(packed.at[pl.ds(at, 4 * CELL), :], o_ref.at[pl.ds(at, 4 * CELL), :], sem).start()
        return 0

    lax.fori_loop(0, 8, target, 0)
    pltpu.make_async_copy(packed, o_ref, sem).wait()


def attend_kernel(
    group_ref, lengths_ref, assignment_ref, q_ref, k_ref, v_ref, *rest
):
    outs, (qf, kf, vf, o_ref, start_ref, size_ref, seen_ref, sem) = rest[:8], rest[8:]
    cell_tables(group_ref[0], lengths_ref, assignment_ref, start_ref, size_ref, seen_ref)
    rows = q_ref.shape[0]

    def widen(i, _):
        r = pl.multiple_of(i * 128, 128)
        qf[pl.ds(r, 128), :] = q_ref[pl.ds(r, 128), :].astype(F32) * (HD**-0.5)
        kf[pl.ds(r, 128), :] = k_ref[pl.ds(r, 128), :].astype(F32)
        vf[pl.ds(r, 128), :] = v_ref[pl.ds(r, 128), :].astype(F32)
        return 0

    lax.fori_loop(0, rows // 128, widen, 0)
    for ref in (qf, kf, vf):
        ref[rows : rows + 136, :] = jnp.zeros((136, 128), F32)
    lane = lax.broadcasted_iota(jnp.int32, (CELL, 128), 1)
    low = lane < 64
    frame = 4 * lax.broadcasted_iota(jnp.int32, (CELL, 128), 0) + lane // 64
    lane2 = lax.broadcasted_iota(jnp.int32, (2 * CELL, 128), 1)
    low2 = lane2 < 64
    column = lax.broadcasted_iota(jnp.int32, (1, MAXLEN), 1)
    key_frame = 2 * (column % 128) + column // 128

    def doubled(ref, row, shift):
        now = ref[pl.ds(row, 2 * CELL), :]
        later = ref[pl.ds(row + 1, 2 * CELL), :]
        even = jnp.where(lane2 >= shift, now, later)
        other = pltpu.roll(even, 64, 1)
        swap = shift > 0
        first = jnp.where(low2, even, other)
        second = jnp.where(low2, other, even)
        return jnp.concatenate(
            [jnp.where(swap, second, first), jnp.where(swap, first, second)], axis=0
        ).astype(BF16)

    def scored(c):
        b = start_ref[c]
        n = size_ref[c]
        row = b // 2
        shift = 64 * (b - 2 * row)
        u0 = qf[pl.ds(row, CELL, stride=2), :]
        u1 = qf[pl.ds(row + 1, CELL, stride=2), :]
        u2 = qf[pl.ds(row + 2, CELL, stride=2), :]
        v0 = pltpu.roll(jnp.where(lane >= shift, u0, u1), shift, 1)
        v1 = pltpu.roll(jnp.where(lane >= shift, u1, u2), shift, 1)
        queries = jnp.concatenate(
            [
                jnp.where(low, v0, 0.0),
                jnp.where(low, 0.0, v0),
                jnp.where(low, v1, 0.0),
                jnp.where(low, 0.0, v1),
            ],
            axis=0,
        ).astype(BF16)
        keys = doubled(kf, row, shift)
        values = doubled(vf, row, shift)
        return n, values, lax.dot_general(queries, keys, NT, preferred_element_type=F32)

    def weighted(n, scores):
        scores = jnp.where(key_frame < n, scores, MASKED)
        exponentials = jnp.exp(scores - jnp.max(scores, axis=1, keepdims=True))
        total = jnp.sum(exponentials, axis=1, keepdims=True)
        return exponentials.astype(BF16), total

    def store(c, n, values, exponentials, total):
        context = jnp.dot(exponentials, values, preferred_element_type=F32) * (1.0 / total)
        at = pl.multiple_of(c * CELL, CELL)
        first = jnp.where(low, context[0:64], context[64:128])
        second = jnp.where(low, context[128:192], context[192:256])
        o_ref[pl.ds(at, CELL), 0:128] = jnp.where(frame < n, first, 0.0).astype(BF16)
        o_ref[pl.ds(at, CELL), 128:256] = jnp.where(frame + 2 < n, second, 0.0).astype(BF16)

    def some(i, _):
        cells = [4 * i + c for c in range(4)]
        work = [scored(c) for c in cells]
        shares = [weighted(n, scores) for n, _, scores in work]
        for c, (n, values, _), share in zip(cells, work, shares):
            store(c, n, values, *share)
        return 0

    lax.fori_loop(0, 8, some, 0)
    copies = []
    for s in range(8):
        at = pl.multiple_of((group_ref[0] ^ s) * 4 * CELL, 4 * CELL)
        copies.append(pltpu.make_async_copy(o_ref.at[pl.ds(at, 4 * CELL), :], outs[s], sem.at[s]))
    for copy in copies:
        copy.start()
    for copy in copies:
        copy.wait()


def compact_kernel(width, offset, count, group_ref, after_ref, *rest):
    parts, (o_ref, flat, windows, sem) = rest[:count], rest[-4:]
    lanes = 4 * width
    blocks = lanes // 128
    total = flat.shape[1]
    slabs = o_ref.shape[0]

    def clear(i, _):
        r = pl.multiple_of(i * 16, 16)
        for b in range(blocks):
            flat[b, pl.ds(r, 16), :] = jnp.zeros((16, 128), F32)
        return 0

    lax.fori_loop(0, total // 16, clear, 0, unroll=7)
    lane = lax.broadcasted_iota(jnp.int32, (CELL, lanes), 1)

    def cell(block, first):
        row = first // 4
        phase = first - 4 * row
        block = block.astype(F32)
        block = jnp.where(phase >= 2, turn(block, lanes - 2 * width), block)
        block = jnp.where(phase % 2 == 1, turn(block, lanes - width), block)
        own = lane >= phase * width
        return row, jnp.where(own, block, 0.0), jnp.where(own, 0.0, block)

    def four(x_ref, at, u):
        moved = [cell(x_ref[pl.ds(at + k * CELL, CELL), :], after_ref[u + k]) for k in range(4)]
        for row, here, below in moved:
            for b in range(blocks):
                at = (b, pl.ds(row + 8, CELL), slice(None))
                flat[at] = flat[at] + here[:, 128 * b : 128 * b + 128]
            for b in range(blocks):
                at = (b, pl.ds(row + 9, CELL), slice(None))
                flat[at] = flat[at] + below[:, 128 * b : 128 * b + 128]

    if count == 1:

        def some(d, _):
            four(parts[0], pl.multiple_of(4 * CELL * d, 4 * CELL), 4 * d)
            return 0

        lax.fori_loop(0, 8, some, 0)
    else:
        for s, part in enumerate(parts):
            four(part, 0, 4 * (group_ref[0] ^ s))

    def window(m, _):
        for b in range(blocks):
            windows[m, :, 128 * b : 128 * b + 128] = flat[b, pl.ds(pl.multiple_of(m * 128, 128), 144), :].astype(BF16)
        pltpu.make_async_copy(windows.at[m], o_ref.at[m, :, pl.ds(offset, lanes)], sem).start()
        return 0

    lax.fori_loop(0, slabs, window, 0)
    pltpu.make_async_copy(windows, o_ref.at[:, :, pl.ds(offset, lanes)], sem).wait()


WIN = 144
EDGE = 8


def rest_kernel(
    slab_ref,
    ends_ref,
    x_ref,
    w_ref,
    gain_ref,
    bias_ref,
    taps_ref,
    scale_ref,
    shift_ref,
    o_ref,
    wo,
    wg,
    wd,
    ctx,
    carried,
    normed,
    gated,
    segment,
    sums,
    swished,
    turned,
    sems,
):
    slab = slab_ref[0]
    piece = 176

    def fetch(g, _):
        c = g // 16
        m = g - 16 * c
        base = pl.multiple_of(g * piece, 16)
        for s in range(3):
            pltpu.make_async_copy(
                w_ref.at[pl.ds(base, 32), pl.ds(512 * s, 512)],
                wo.at[pl.ds(pl.multiple_of(96 * m + 32 * s, 16), 32), pl.ds(pl.multiple_of(512 * c, 512), 512)],
                sems.at[0],
            ).start()
        return 0

    def fetch_glu(half):
        def one(i, _):
            c = i // 8
            m = 4 * half + i % 4 + 8 * ((i // 4) % 2)
            base = pl.multiple_of((16 * c + m) * piece + 32, 16)
            pltpu.make_async_copy(
                w_ref.at[pl.ds(base, 96), :],
                wg.at[pl.ds(pl.multiple_of(192 * m + 96 * c, 16), 96), :],
                sems.at[1 + half],
            ).start()
            return 0

        lax.fori_loop(0, 16, one, 0)

    def fetch_down(g, _):
        c = g // 16
        m = g - 16 * c
        base = pl.multiple_of(g * piece + 128, 16)
        pltpu.make_async_copy(
            w_ref.at[pl.ds(base, 48), :],
            wd.at[pl.ds(pl.multiple_of(96 * m + 48 * c, 16), 48), :],
            sems.at[3],
        ).start()
        return 0

    lax.fori_loop(0, 32, fetch, 0)
    fetch_glu(0)
    fetch_glu(1)
    lax.fori_loop(0, 32, fetch_down, 0)

    for j in range(4):
        frame = 512 * slab - 4 * EDGE + j + 4 * lax.broadcasted_iota(jnp.int32, (WIN, 128), 0)

        def count(i, number):
            return number + jnp.where(frame >= ends_ref[i], 1, 0)

        number = lax.fori_loop(0, 32, count, jnp.where(frame >= 0, 0, -1), unroll=4)
        segment[j] = number.astype(F32)

    lane = lax.broadcasted_iota(jnp.int32, (WIN, 384), 1)

    def features(g, _):
        at = pl.ds(pl.multiple_of(384 * g, 128), 384)
        for j in range(4):
            whole = None
            for f in range(4):
                s = 96 * ((f - j) % 4)
                block = x_ref[4 * g + f, :, 0:384]
                if s:
                    block = turn(block, 384 - s)
                whole = block if whole is None else jnp.where(lane >= 96 * f, block, whole)
            carried[WIN * j : WIN * j + WIN, at] = whole.astype(F32)
        return 0

    lax.fori_loop(0, 4, features, 0)

    low = lax.broadcasted_iota(jnp.int32, (WIN, 128), 1) < 64

    def heads(h, _):
        at = pl.ds(pl.multiple_of(128 * h, 128), 128)
        for j in range(4):
            part = slice(384 + 128 * (j // 2), 512 + 128 * (j // 2))
            left = x_ref[2 * h, :, part].astype(F32)
            right = x_ref[2 * h + 1, :, part].astype(F32)
            if j % 2 == 0:
                right = pltpu.roll(right, 64, 1)
            else:
                left = pltpu.roll(left, 64, 1)
            ctx[WIN * j : WIN * j + WIN, at] = jnp.where(low, left, right).astype(BF16)
        return 0

    lax.fori_loop(0, 8, heads, 0)

    pltpu.make_async_copy(wo, wo, sems.at[0]).wait()

    def project(n, _):
        at = pl.ds(pl.multiple_of(256 * n, 256), 256)
        carried[:, at] = carried[:, at] + lax.dot_general(
            ctx[...], wo[at, :], NT, preferred_element_type=F32
        )
        return 0

    lax.fori_loop(0, 6, project, 0)

    def norm(i, _):
        at = pl.ds(pl.multiple_of(16 * i, 16), 16)
        rows = carried[at, :]
        centred = rows - jnp.mean(rows, axis=1, keepdims=True)
        variance = jnp.mean(centred * centred, axis=1, keepdims=True)
        normed[at, :] = (centred * lax.rsqrt(variance + EPS) * gain_ref[...] + bias_ref[...]).astype(BF16)
        return 0

    lax.fori_loop(0, 4 * WIN // 16, norm, 0, unroll=4)

    def glu(n, _):
        value = lax.dot_general(
            normed[...], wg[pl.ds(pl.multiple_of(256 * n, 256), 256), :], NT, preferred_element_type=F32
        )
        gate = lax.dot_general(
            normed[...], wg[pl.ds(pl.multiple_of(1536 + 256 * n, 256), 256), :], NT, preferred_element_type=F32
        )
        out = (value * jax.nn.sigmoid(gate)).astype(BF16).astype(F32)
        for j in range(4):
            for b in range(2):
                gated[2 * n + b, j] = out[WIN * j : WIN * j + WIN, 128 * b : 128 * b + 128]
        return 0

    for half in range(2):
        part = wg.at[pl.ds(0, 1536), :]
        pltpu.make_async_copy(part, part, sems.at[1 + half]).wait()
        lax.fori_loop(3 * half, 3 * half + 3, glu, 0)

    def conv(b, _):
        lanes = [pl.ds(pl.multiple_of(512 * b + 128 * l, 128), 128) for l in range(4)]
        for first, last in ((-15, -8), (-7, 0), (1, 8), (9, 15)):
            taps = [
                {o: jnp.broadcast_to(taps_ref[o + HALF : o + HALF + 1, at], (8, 128)) for o in range(first, last + 1)}
                for at in lanes
            ]

            def chunk(i, _):
                row = EDGE + i * 8
                for pair in ((0, 1), (2, 3)):
                    mine = {j: segment[j, pl.ds(pl.multiple_of(row, 8), 8), :] for j in pair}
                    rows = {j: pl.ds(pl.multiple_of(128 * j + 8 * i, 8), 8) for j in pair}
                    total = {(l, j): None if first == -15 else sums[l, rows[j], :] for l in range(4) for j in pair}
                    for e in range(first + pair[0], last + pair[1] + 1):
                        d, p = e // 4, e % 4
                        values = [gated[4 * b + l, p, pl.ds(row + d, 8), :] for l in range(4)]
                        owner = segment[p, pl.ds(row + d, 8), :]
                        for j in pair:
                            if not first <= e - j <= last:
                                continue
                            same = owner == mine[j]
                            for l in range(4):
                                term = jnp.where(same, values[l], 0.0) * taps[l][e - j]
                                total[l, j] = term if total[l, j] is None else total[l, j] + term
                    for j in pair:
                        for l in range(4):
                            sums[l, rows[j], :] = total[l, j]
                return 0

            lax.fori_loop(0, 16, chunk, 0)
        for l, at in enumerate(lanes):
            affine = sums[l] * scale_ref[:, at] + shift_ref[:, at]
            swished[:, at] = (affine * jax.nn.sigmoid(affine)).astype(BF16)
        return 0

    lax.fori_loop(0, 3, conv, 0)

    pltpu.make_async_copy(wd, wd, sems.at[3]).wait()
    live = ends_ref[31]

    def down(n, _):
        at = pl.ds(pl.multiple_of(256 * n, 256), 256)
        lowered = lax.dot_general(swished[...], wd[at, :], NT, preferred_element_type=F32)
        for j in range(4):
            frame = 512 * slab + j + 4 * lax.broadcasted_iota(jnp.int32, (128, 256), 0)
            rows = carried[WIN * j + EDGE : WIN * j + EDGE + 128, at] + lowered[128 * j : 128 * j + 128]
            rows = jnp.where(frame < live, rows, 0.0)
            for b in range(2):
                turned[b, pl.ds(j, 128, stride=4), :] = rows[:, 128 * b : 128 * b + 128]
        o_ref[:, at] = jnp.concatenate([turned[0], turned[1]], axis=1).astype(BF16)
        return 0

    lax.fori_loop(0, 6, down, 0)


HBM = pl.BlockSpec(memory_space=pltpu.HBM)
SMEM = pl.BlockSpec(memory_space=pltpu.SMEM)
VMEM = pl.BlockSpec(memory_space=pltpu.VMEM)
BIG = 60 * 1024 * 1024


def pack(group, lengths, assignment, x):
    rows = x.shape[0]
    return pl.pallas_call(
        pack_kernel,
        out_shape=jax.ShapeDtypeStruct((32 * CELL, 384), BF16),
        in_specs=[SMEM, SMEM, SMEM, VMEM],
        out_specs=HBM,
        scratch_shapes=[
            pltpu.VMEM((3, rows + 72, 128), F32),
            pltpu.VMEM((32 * CELL, 384), BF16),
            pltpu.SMEM((32,), jnp.int32),
            pltpu.SMEM((32,), jnp.int32),
            pltpu.SMEM((8,), jnp.int32),
            pltpu.SemaphoreType.DMA,
        ],
        compiler_params=pltpu.CompilerParams(vmem_limit_bytes=24 * 1024 * 1024),
        cost_estimate=pl.CostEstimate(flops=20_000_000, bytes_accessed=3_200_000, transcendentals=0),
        name="pack_cells",
    )(group, lengths, assignment, x)


def attend(group, lengths, assignment, q, k, v):
    rows = q.shape[0]
    return pl.pallas_call(
        attend_kernel,
        out_shape=[jax.ShapeDtypeStruct((4 * CELL, 256), BF16)] * 8,
        in_specs=[SMEM, SMEM, SMEM, VMEM, VMEM, VMEM],
        out_specs=[HBM] * 8,
        scratch_shapes=[
            pltpu.VMEM((rows + 136, 128), F32),
            pltpu.VMEM((rows + 136, 128), F32),
            pltpu.VMEM((rows + 136, 128), F32),
            pltpu.VMEM((32 * CELL, 256), BF16),
            pltpu.SMEM((32,), jnp.int32),
            pltpu.SMEM((32,), jnp.int32),
            pltpu.SMEM((8,), jnp.int32),
            pltpu.SemaphoreType.DMA((8,)),
        ],
        compiler_params=pltpu.CompilerParams(vmem_limit_bytes=32 * 1024 * 1024),
        cost_estimate=pl.CostEstimate(flops=2_000_000_000, bytes_accessed=4_200_000, transcendentals=2_000_000),
        name="attend_cells",
    )(group, lengths, assignment, q, k, v)


def compact(width, offset, group, after, cells, slabs, onto=None):
    lanes = 4 * width
    return pl.pallas_call(
        functools.partial(compact_kernel, width, offset, len(cells)),
        out_shape=jax.ShapeDtypeStruct((slabs, WIN, 640), BF16),
        in_specs=[SMEM, SMEM] + [VMEM] * len(cells) + ([] if onto is None else [HBM]),
        out_specs=HBM,
        scratch_shapes=[
            pltpu.VMEM((lanes // 128, 32 * CELL + 80, 128), F32),
            pltpu.VMEM((slabs, WIN, lanes), BF16),
            pltpu.SemaphoreType.DMA,
        ],
        input_output_aliases={} if onto is None else {2 + len(cells): 0},
        compiler_params=pltpu.CompilerParams(vmem_limit_bytes=24 * 1024 * 1024),
        cost_estimate=pl.CostEstimate(flops=20_000_000, bytes_accessed=3_200_000, transcendentals=0),
        name="compact_cells",
    )(group, after, *cells, *([] if onto is None else [onto]))


def rest(slab, ends, x, w, gain, bias, taps, scale, shift):
    return pl.pallas_call(
        rest_kernel,
        out_shape=jax.ShapeDtypeStruct((512, 1536), BF16),
        in_specs=[SMEM, SMEM, VMEM, HBM] + [VMEM] * 5,
        out_specs=VMEM,
        scratch_shapes=[
            pltpu.VMEM((1536, 1024), BF16),
            pltpu.VMEM((3072, 1536), BF16),
            pltpu.VMEM((1536, 1536), BF16),
            pltpu.VMEM((4 * WIN, 1024), BF16),
            pltpu.VMEM((4 * WIN, 1536), F32),
            pltpu.VMEM((4 * WIN, 1536), BF16),
            pltpu.VMEM((12, 4, WIN, 128), F32),
            pltpu.VMEM((4, WIN, 128), F32),
            pltpu.VMEM((4, 512, 128), F32),
            pltpu.VMEM((512, 1536), BF16),
            pltpu.VMEM((2, 512, 128), F32),
            pltpu.SemaphoreType.DMA((4,)),
        ],
        compiler_params=pltpu.CompilerParams(vmem_limit_bytes=BIG),
        cost_estimate=pl.CostEstimate(flops=9_000_000_000, bytes_accessed=25_000_000, transcendentals=2_000_000),
        name="project_and_convolve",
    )(slab, ends, x, w, gain, bias, taps, scale, shift)


def target_tables(data_group, lengths, assignment):
    count = lengths.shape[0]
    number = jnp.arange(count, dtype=jnp.int32)
    mine = assignment == data_group
    place = jnp.sum(jnp.where((number[None, :] < number[:, None]) & mine[None, :], 1, 0), axis=1)
    slot = jnp.arange(32, dtype=jnp.int32)
    spans = jnp.sum(jnp.where(mine[None, :] & (place[None, :] == slot[:, None]), lengths[None, :], 0), axis=1)
    first = jnp.sum(jnp.where(slot[None, :] < slot[:, None], spans[None, :], 0), axis=1)
    return first, first + spans


def on_device(
    query_rows,
    key_rows,
    value_rows,
    residual,
    lengths,
    assignment,
    out_proj,
    norm_gain,
    norm_bias,
    glu_proj,
    conv_taps,
    batch_scale,
    batch_shift,
    down_proj,
):
    data_group = lax.axis_index("dp").astype(jnp.int32)
    slab = lax.axis_index("mp").astype(jnp.int32)
    groups = lax.axis_size("dp")
    slabs = lax.axis_size("mp")
    core = data_group % 2
    op = lax.dynamic_slice_in_dim(out_proj.T, core * 512, 512, 1)
    op = jnp.concatenate([op[0:32], op[32:64], op[64:96]], axis=1)
    glu = lax.dynamic_slice_in_dim(glu_proj.T, core * 96, 96, 0)
    dn = lax.dynamic_slice_in_dim(down_proj.T, core * 48, 48, 0)
    mine = jnp.concatenate([op, glu, dn], axis=0)
    chips = [[(2 * p + c) * slabs + m for c in range(2) for m in range(slabs)] for p in range(groups // 2)]
    weights = lax.all_gather(mine, ("dp", "mp"), axis=0, tiled=True, axis_index_groups=chips)

    group = data_group.reshape(1)
    x_cells = pack(group, lengths, assignment, residual.reshape(residual.shape[0], 384))
    x_here = lax.all_to_all(
        x_cells.reshape(groups, 4 * CELL, 384), "dp", split_axis=0, concat_axis=0, tiled=True
    )
    group_later, _ = lax.optimization_barrier((group, x_cells))
    c_cells = attend(
        group_later,
        lengths,
        assignment,
        query_rows.reshape(-1, 128),
        key_rows.reshape(-1, 128),
        value_rows.reshape(-1, 128),
    )
    x_here, first_cells = lax.optimization_barrier((x_here, c_cells[0]))
    c_here = [first_cells] + [
        lax.ppermute(c_cells[s], "dp", [(i, i ^ s) for i in range(groups)]) for s in range(1, groups)
    ]
    first, ends = target_tables(data_group, lengths, assignment)
    windows = compact(96, 0, group, first, [x_here.reshape(-1, 384)], slabs)
    windows = compact(64, 384, group, first, c_here, slabs, onto=windows)
    slab_rows = lax.all_to_all(windows, "mp", split_axis=0, concat_axis=0, tiled=True)
    row = lambda a: a.reshape(1, -1)
    return rest(
        slab.reshape(1),
        ends,
        slab_rows,
        weights,
        row(norm_gain),
        row(norm_bias),
        conv_taps,
        row(batch_scale),
        row(batch_shift),
    )


def solution(mesh):
    in_specs = (
        P("dp", "mp", None),
        P("dp", "mp", None),
        P("dp", "mp", None),
        P("dp", "mp", None),
        P(),
        P(),
        P(None, "mp"),
        P(),
        P(),
        P(None, "mp"),
        P(),
        P(),
        P(),
        P(None, "mp"),
    )
    out_specs = P(("dp", "mp"), None)
    return jax.shard_map(
        on_device, mesh=mesh, in_specs=in_specs, out_specs=out_specs, check_vma=False
    )
```

```python
import functools

import jax
import jax.numpy as jnp
from jax import lax
from jax.experimental import pallas as pl
from jax.experimental.pallas import tpu as pltpu
from jax.sharding import PartitionSpec as P

HD = 64
KERNEL = 31
HALF = 15
MAXLEN = 256
EPS = 1e-05
MASKED = -1e30

CELL = MAXLEN // 4
F32 = jnp.float32
BF16 = jnp.bfloat16
NT = (((1,), (1,)), ((), ()))


def cell_tables(data_group, lengths_ref, assignment_ref, start_ref, size_ref, seen_ref):
    per_group = 32
    for t in range(8):
        seen_ref[t] = 0

    def step(i, at):
        u = data_group * per_group + i
        t = assignment_ref[u]
        n = lengths_ref[u]
        k = seen_ref[t]
        seen_ref[t] = k + 1
        start_ref[4 * t + k] = at
        size_ref[4 * t + k] = n
        return at + n

    lax.fori_loop(0, per_group, step, jnp.int32(0))


def turn(x, s):
    return jnp.concatenate([x[:, s:], x[:, :s]], axis=1)


def pack_kernel(
    group_ref, lengths_ref, assignment_ref, x_ref, o_ref, flat, packed, start_ref, size_ref, seen_ref, sem
):
    cell_tables(group_ref[0], lengths_ref, assignment_ref, start_ref, size_ref, seen_ref)
    rows = x_ref.shape[0]

    def widen(i, _):
        r = pl.multiple_of(i * 64, 64)
        for b in range(3):
            flat[b, pl.ds(r, 64), :] = x_ref[pl.ds(r, 64), 128 * b : 128 * b + 128].astype(F32)
        return 0

    lax.fori_loop(0, rows // 64, widen, 0)
    for b in range(3):
        flat[b, rows : rows + 72, :] = jnp.zeros((72, 128), F32)
    lane = lax.broadcasted_iota(jnp.int32, (CELL, 384), 1)
    frame = 4 * lax.broadcasted_iota(jnp.int32, (CELL, 384), 0) + lane // 96

    def cell(c):
        b = start_ref[c]
        row = b // 4
        phase = b - 4 * row
        now = jnp.concatenate([flat[i, pl.ds(row, CELL), :] for i in range(3)], axis=1)
        later = jnp.concatenate([flat[i, pl.ds(row + 1, CELL), :] for i in range(3)], axis=1)
        mixed = jnp.where(lane >= 96 * phase, now, later)
        mixed = jnp.where(phase >= 2, turn(mixed, 192), mixed)
        mixed = jnp.where(phase % 2 == 1, turn(mixed, 96), mixed)
        return jnp.where(frame < size_ref[c], mixed, 0.0).astype(BF16)

    def target(t, _):
        parts = [cell(4 * t + k) for k in range(4)]
        at = pl.multiple_of(4 * CELL * t, 4 * CELL)
        for k, part in enumerate(parts):
            packed[pl.ds(at + k * CELL, CELL), :] = part
        pltpu.make_async_copy(packed.at[pl.ds(at, 4 * CELL), :], o_ref.at[pl.ds(at, 4 * CELL), :], sem).start()
        return 0

    lax.fori_loop(0, 8, target, 0)
    pltpu.make_async_copy(packed, o_ref, sem).wait()


def attend_kernel(
    group_ref, lengths_ref, assignment_ref, q_ref, k_ref, v_ref, *rest
):
    outs, (qf, kf, vf, o_ref, start_ref, size_ref, seen_ref, sem) = rest[:8], rest[8:]
    cell_tables(group_ref[0], lengths_ref, assignment_ref, start_ref, size_ref, seen_ref)
    rows = q_ref.shape[0]

    def widen(i, _):
        r = pl.multiple_of(i * 128, 128)
        qf[pl.ds(r, 128), :] = q_ref[pl.ds(r, 128), :].astype(F32) * (HD**-0.5)
        kf[pl.ds(r, 128), :] = k_ref[pl.ds(r, 128), :].astype(F32)
        vf[pl.ds(r, 128), :] = v_ref[pl.ds(r, 128), :].astype(F32)
        return 0

    lax.fori_loop(0, rows // 128, widen, 0)
    for ref in (qf, kf, vf):
        ref[rows : rows + 136, :] = jnp.zeros((136, 128), F32)
    lane = lax.broadcasted_iota(jnp.int32, (CELL, 128), 1)
    low = lane < 64
    frame = 4 * lax.broadcasted_iota(jnp.int32, (CELL, 128), 0) + lane // 64
    lane2 = lax.broadcasted_iota(jnp.int32, (2 * CELL, 128), 1)
    low2 = lane2 < 64
    column = lax.broadcasted_iota(jnp.int32, (1, MAXLEN), 1)
    key_frame = 2 * (column % 128) + column // 128

    def doubled(ref, row, shift):
        now = ref[pl.ds(row, 2 * CELL), :]
        later = ref[pl.ds(row + 1, 2 * CELL), :]
        even = jnp.where(lane2 >= shift, now, later)
        other = pltpu.roll(even, 64, 1)
        swap = shift > 0
        first = jnp.where(low2, even, other)
        second = jnp.where(low2, other, even)
        return jnp.concatenate(
            [jnp.where(swap, second, first), jnp.where(swap, first, second)], axis=0
        ).astype(BF16)

    def scored(c):
        b = start_ref[c]
        n = size_ref[c]
        row = b // 2
        shift = 64 * (b - 2 * row)
        u0 = qf[pl.ds(row, CELL, stride=2), :]
        u1 = qf[pl.ds(row + 1, CELL, stride=2), :]
        u2 = qf[pl.ds(row + 2, CELL, stride=2), :]
        v0 = pltpu.roll(jnp.where(lane >= shift, u0, u1), shift, 1)
        v1 = pltpu.roll(jnp.where(lane >= shift, u1, u2), shift, 1)
        queries = jnp.concatenate(
            [
                jnp.where(low, v0, 0.0),
                jnp.where(low, 0.0, v0),
                jnp.where(low, v1, 0.0),
                jnp.where(low, 0.0, v1),
            ],
            axis=0,
        ).astype(BF16)
        keys = doubled(kf, row, shift)
        values = doubled(vf, row, shift)
        return n, values, lax.dot_general(queries, keys, NT, preferred_element_type=F32)

    def weighted(n, scores):
        scores = jnp.where(key_frame < n, scores, MASKED)
        exponentials = jnp.exp(scores - jnp.max(scores, axis=1, keepdims=True))
        total = jnp.sum(exponentials, axis=1, keepdims=True)
        return exponentials.astype(BF16), total

    def store(c, n, values, exponentials, total):
        context = jnp.dot(exponentials, values, preferred_element_type=F32) * (1.0 / total)
        at = pl.multiple_of(c * CELL, CELL)
        first = jnp.where(low, context[0:64], context[64:128])
        second = jnp.where(low, context[128:192], context[192:256])
        o_ref[pl.ds(at, CELL), 0:128] = jnp.where(frame < n, first, 0.0).astype(BF16)
        o_ref[pl.ds(at, CELL), 128:256] = jnp.where(frame + 2 < n, second, 0.0).astype(BF16)

    def some(i, _):
        cells = [4 * i + c for c in range(4)]
        work = [scored(c) for c in cells]
        shares = [weighted(n, scores) for n, _, scores in work]
        for c, (n, values, _), share in zip(cells, work, shares):
            store(c, n, values, *share)
        return 0

    lax.fori_loop(0, 8, some, 0)
    copies = []
    for s in range(8):
        at = pl.multiple_of((group_ref[0] ^ s) * 4 * CELL, 4 * CELL)
        copies.append(pltpu.make_async_copy(o_ref.at[pl.ds(at, 4 * CELL), :], outs[s], sem.at[s]))
    for copy in copies:
        copy.start()
    for copy in copies:
        copy.wait()


def compact_kernel(width, offset, count, group_ref, after_ref, *rest):
    parts, (o_ref, flat, windows, sem) = rest[:count], rest[-4:]
    lanes = 4 * width
    blocks = lanes // 128
    total = flat.shape[1]
    slabs = o_ref.shape[0]

    def clear(i, _):
        r = pl.multiple_of(i * 16, 16)
        for b in range(blocks):
            flat[b, pl.ds(r, 16), :] = jnp.zeros((16, 128), F32)
        return 0

    lax.fori_loop(0, total // 16, clear, 0, unroll=7)
    lane = lax.broadcasted_iota(jnp.int32, (CELL, lanes), 1)

    def cell(block, first):
        row = first // 4
        phase = first - 4 * row
        block = block.astype(F32)
        block = jnp.where(phase >= 2, turn(block, lanes - 2 * width), block)
        block = jnp.where(phase % 2 == 1, turn(block, lanes - width), block)
        own = lane >= phase * width
        return row, jnp.where(own, block, 0.0), jnp.where(own, 0.0, block)

    def four(x_ref, at, u):
        moved = [cell(x_ref[pl.ds(at + k * CELL, CELL), :], after_ref[u + k]) for k in range(4)]
        for row, here, below in moved:
            for b in range(blocks):
                at = (b, pl.ds(row + 8, CELL), slice(None))
                flat[at] = flat[at] + here[:, 128 * b : 128 * b + 128]
            for b in range(blocks):
                at = (b, pl.ds(row + 9, CELL), slice(None))
                flat[at] = flat[at] + below[:, 128 * b : 128 * b + 128]

    if count == 1:

        def some(d, _):
            four(parts[0], pl.multiple_of(4 * CELL * d, 4 * CELL), 4 * d)
            return 0

        lax.fori_loop(0, 8, some, 0)
    else:
        for s, part in enumerate(parts):
            four(part, 0, 4 * (group_ref[0] ^ s))

    def window(m, _):
        for b in range(blocks):
            windows[m, :, 128 * b : 128 * b + 128] = flat[b, pl.ds(pl.multiple_of(m * 128, 128), 144), :].astype(BF16)
        pltpu.make_async_copy(windows.at[m], o_ref.at[m, :, pl.ds(offset, lanes)], sem).start()
        return 0

    lax.fori_loop(0, slabs, window, 0)
    pltpu.make_async_copy(windows, o_ref.at[:, :, pl.ds(offset, lanes)], sem).wait()


WIN = 144
EDGE = 8


def rest_kernel(
    slab_ref,
    ends_ref,
    x_ref,
    w_ref,
    gain_ref,
    bias_ref,
    taps_ref,
    scale_ref,
    shift_ref,
    o_ref,
    wo,
    wg,
    wd,
    ctx,
    carried,
    normed,
    gated,
    segment,
    sums,
    swished,
    turned,
    sems,
):
    slab = slab_ref[0]
    wo3, wg3, wd3 = wo.reshape(16, 96, 1024), wg.reshape(16, 192, 1536), wd.reshape(16, 96, 1536)
    rows = [pl.ds(48 * i, 48) for i in range(4)]
    for e in range(8):
        pltpu.make_async_copy(
            w_ref.at[e, :, :, pl.ds(768, 256)], wo3.at[:, rows[e % 2], pl.ds(256 * (e // 2), 256)], sems.at[0]
        ).start()
    for half in range(2):
        for e in range(8):
            for first in (4 * half, 8 + 4 * half):
                pltpu.make_async_copy(
                    w_ref.at[e, pl.ds(first, 4), :, pl.ds(0, 768)],
                    wg3.at[pl.ds(first, 4), rows[e % 4], pl.ds(768 * (e // 4), 768)],
                    sems.at[1 + half],
                ).start()
    for e in range(8):
        pltpu.make_async_copy(
            w_ref.at[e, :, :, pl.ds(1024, 384)], wd3.at[:, rows[e % 2], pl.ds(384 * (e // 2), 384)], sems.at[3]
        ).start()

    for j in range(4):
        frame = 512 * slab - 4 * EDGE + j + 4 * lax.broadcasted_iota(jnp.int32, (WIN, 128), 0)

        def count(i, number):
            return number + jnp.where(frame >= ends_ref[i], 1, 0)

        number = lax.fori_loop(0, 32, count, jnp.where(frame >= 0, 0, -1), unroll=4)
        segment[j] = number.astype(F32)

    lane = lax.broadcasted_iota(jnp.int32, (WIN, 384), 1)

    def features(g, _):
        at = pl.ds(pl.multiple_of(384 * g, 128), 384)
        for j in range(4):
            whole = None
            for f in range(4):
                s = 96 * ((f - j) % 4)
                block = x_ref[4 * g + f, :, 0:384]
                if s:
                    block = turn(block, 384 - s)
                whole = block if whole is None else jnp.where(lane >= 96 * f, block, whole)
            carried[WIN * j : WIN * j + WIN, at] = whole.astype(F32)
        return 0

    lax.fori_loop(0, 4, features, 0)

    low = lax.broadcasted_iota(jnp.int32, (WIN, 128), 1) < 64

    def heads(h, _):
        at = pl.ds(pl.multiple_of(128 * h, 128), 128)
        for j in range(4):
            part = slice(384 + 128 * (j // 2), 512 + 128 * (j // 2))
            left = x_ref[2 * h, :, part].astype(F32)
            right = x_ref[2 * h + 1, :, part].astype(F32)
            if j % 2 == 0:
                right = pltpu.roll(right, 64, 1)
            else:
                left = pltpu.roll(left, 64, 1)
            ctx[WIN * j : WIN * j + WIN, at] = jnp.where(low, left, right).astype(BF16)
        return 0

    lax.fori_loop(0, 8, heads, 0)

    pltpu.make_async_copy(wo, wo, sems.at[0]).wait()

    def project(n, _):
        at = pl.ds(pl.multiple_of(256 * n, 256), 256)
        carried[:, at] = carried[:, at] + lax.dot_general(
            ctx[...], wo[at, :], NT, preferred_element_type=F32
        )
        return 0

    lax.fori_loop(0, 6, project, 0)

    def norm(i, _):
        at = pl.ds(pl.multiple_of(16 * i, 16), 16)
        rows = carried[at, :]
        centred = rows - jnp.mean(rows, axis=1, keepdims=True)
        variance = jnp.mean(centred * centred, axis=1, keepdims=True)
        normed[at, :] = (centred * lax.rsqrt(variance + EPS) * gain_ref[...] + bias_ref[...]).astype(BF16)
        return 0

    lax.fori_loop(0, 4 * WIN // 16, norm, 0, unroll=4)

    def glu(n, _):
        value = lax.dot_general(
            normed[...], wg[pl.ds(pl.multiple_of(256 * n, 256), 256), :], NT, preferred_element_type=F32
        )
        gate = lax.dot_general(
            normed[...], wg[pl.ds(pl.multiple_of(1536 + 256 * n, 256), 256), :], NT, preferred_element_type=F32
        )
        out = (value * jax.nn.sigmoid(gate)).astype(BF16).astype(F32)
        for j in range(4):
            for b in range(2):
                gated[2 * n + b, j] = out[WIN * j : WIN * j + WIN, 128 * b : 128 * b + 128]
        return 0

    for half in range(2):
        part = wg.at[pl.ds(0, 1536), :]
        pltpu.make_async_copy(part, part, sems.at[1 + half]).wait()
        lax.fori_loop(3 * half, 3 * half + 3, glu, 0)

    def conv(b, _):
        lanes = [pl.ds(pl.multiple_of(512 * b + 128 * l, 128), 128) for l in range(4)]
        for first, last in ((-15, -8), (-7, 0), (1, 8), (9, 15)):
            taps = [
                {o: jnp.broadcast_to(taps_ref[o + HALF : o + HALF + 1, at], (8, 128)) for o in range(first, last + 1)}
                for at in lanes
            ]

            def chunk(i, _):
                row = EDGE + i * 8
                for pair in ((0, 1), (2, 3)):
                    mine = {j: segment[j, pl.ds(pl.multiple_of(row, 8), 8), :] for j in pair}
                    rows = {j: pl.ds(pl.multiple_of(128 * j + 8 * i, 8), 8) for j in pair}
                    total = {(l, j): None if first == -15 else sums[l, rows[j], :] for l in range(4) for j in pair}
                    for e in range(first + pair[0], last + pair[1] + 1):
                        d, p = e // 4, e % 4
                        values = [gated[4 * b + l, p, pl.ds(row + d, 8), :] for l in range(4)]
                        owner = segment[p, pl.ds(row + d, 8), :]
                        for j in pair:
                            if not first <= e - j <= last:
                                continue
                            same = owner == mine[j]
                            for l in range(4):
                                term = jnp.where(same, values[l], 0.0) * taps[l][e - j]
                                total[l, j] = term if total[l, j] is None else total[l, j] + term
                    for j in pair:
                        for l in range(4):
                            sums[l, rows[j], :] = total[l, j]
                return 0

            lax.fori_loop(0, 16, chunk, 0)
        for l, at in enumerate(lanes):
            affine = sums[l] * scale_ref[:, at] + shift_ref[:, at]
            swished[:, at] = (affine * jax.nn.sigmoid(affine)).astype(BF16)
        return 0

    lax.fori_loop(0, 3, conv, 0)

    pltpu.make_async_copy(wd, wd, sems.at[3]).wait()
    live = ends_ref[31]

    def down(n, _):
        at = pl.ds(pl.multiple_of(256 * n, 256), 256)
        lowered = lax.dot_general(swished[...], wd[at, :], NT, preferred_element_type=F32)
        for j in range(4):
            frame = 512 * slab + j + 4 * lax.broadcasted_iota(jnp.int32, (128, 256), 0)
            rows = carried[WIN * j + EDGE : WIN * j + EDGE + 128, at] + lowered[128 * j : 128 * j + 128]
            rows = jnp.where(frame < live, rows, 0.0)
            for b in range(2):
                turned[b, pl.ds(j, 128, stride=4), :] = rows[:, 128 * b : 128 * b + 128]
        o_ref[:, at] = jnp.concatenate([turned[0], turned[1]], axis=1).astype(BF16)
        return 0

    lax.fori_loop(0, 6, down, 0)


HBM = pl.BlockSpec(memory_space=pltpu.HBM)
SMEM = pl.BlockSpec(memory_space=pltpu.SMEM)
VMEM = pl.BlockSpec(memory_space=pltpu.VMEM)
BIG = 60 * 1024 * 1024


def pack(group, lengths, assignment, x):
    rows = x.shape[0]
    return pl.pallas_call(
        pack_kernel,
        out_shape=jax.ShapeDtypeStruct((32 * CELL, 384), BF16),
        in_specs=[SMEM, SMEM, SMEM, VMEM],
        out_specs=HBM,
        scratch_shapes=[
            pltpu.VMEM((3, rows + 72, 128), F32),
            pltpu.VMEM((32 * CELL, 384), BF16),
            pltpu.SMEM((32,), jnp.int32),
            pltpu.SMEM((32,), jnp.int32),
            pltpu.SMEM((8,), jnp.int32),
            pltpu.SemaphoreType.DMA,
        ],
        compiler_params=pltpu.CompilerParams(vmem_limit_bytes=24 * 1024 * 1024),
        cost_estimate=pl.CostEstimate(flops=20_000_000, bytes_accessed=3_200_000, transcendentals=0),
        name="pack_cells",
    )(group, lengths, assignment, x)


def attend(group, lengths, assignment, q, k, v):
    rows = q.shape[0]
    return pl.pallas_call(
        attend_kernel,
        out_shape=[jax.ShapeDtypeStruct((4 * CELL, 256), BF16)] * 8,
        in_specs=[SMEM, SMEM, SMEM, VMEM, VMEM, VMEM],
        out_specs=[HBM] * 8,
        scratch_shapes=[
            pltpu.VMEM((rows + 136, 128), F32),
            pltpu.VMEM((rows + 136, 128), F32),
            pltpu.VMEM((rows + 136, 128), F32),
            pltpu.VMEM((32 * CELL, 256), BF16),
            pltpu.SMEM((32,), jnp.int32),
            pltpu.SMEM((32,), jnp.int32),
            pltpu.SMEM((8,), jnp.int32),
            pltpu.SemaphoreType.DMA((8,)),
        ],
        compiler_params=pltpu.CompilerParams(vmem_limit_bytes=32 * 1024 * 1024),
        cost_estimate=pl.CostEstimate(flops=2_000_000_000, bytes_accessed=4_200_000, transcendentals=2_000_000),
        name="attend_cells",
    )(group, lengths, assignment, q, k, v)


def compact(width, offset, group, after, cells, slabs, onto=None):
    lanes = 4 * width
    return pl.pallas_call(
        functools.partial(compact_kernel, width, offset, len(cells)),
        out_shape=jax.ShapeDtypeStruct((slabs, WIN, 640), BF16),
        in_specs=[SMEM, SMEM] + [VMEM] * len(cells) + ([] if onto is None else [HBM]),
        out_specs=HBM,
        scratch_shapes=[
            pltpu.VMEM((lanes // 128, 32 * CELL + 80, 128), F32),
            pltpu.VMEM((slabs, WIN, lanes), BF16),
            pltpu.SemaphoreType.DMA,
        ],
        input_output_aliases={} if onto is None else {2 + len(cells): 0},
        compiler_params=pltpu.CompilerParams(vmem_limit_bytes=24 * 1024 * 1024),
        cost_estimate=pl.CostEstimate(flops=20_000_000, bytes_accessed=3_200_000, transcendentals=0),
        name="compact_cells",
    )(group, after, *cells, *([] if onto is None else [onto]))


def rest(slab, ends, x, w, gain, bias, taps, scale, shift):
    return pl.pallas_call(
        rest_kernel,
        out_shape=jax.ShapeDtypeStruct((512, 1536), BF16),
        in_specs=[SMEM, SMEM, VMEM, HBM] + [VMEM] * 5,
        out_specs=VMEM,
        scratch_shapes=[
            pltpu.VMEM((1536, 1024), BF16),
            pltpu.VMEM((3072, 1536), BF16),
            pltpu.VMEM((1536, 1536), BF16),
            pltpu.VMEM((4 * WIN, 1024), BF16),
            pltpu.VMEM((4 * WIN, 1536), F32),
            pltpu.VMEM((4 * WIN, 1536), BF16),
            pltpu.VMEM((12, 4, WIN, 128), F32),
            pltpu.VMEM((4, WIN, 128), F32),
            pltpu.VMEM((4, 512, 128), F32),
            pltpu.VMEM((512, 1536), BF16),
            pltpu.VMEM((2, 512, 128), F32),
            pltpu.SemaphoreType.DMA((4,)),
        ],
        compiler_params=pltpu.CompilerParams(vmem_limit_bytes=BIG),
        cost_estimate=pl.CostEstimate(flops=9_000_000_000, bytes_accessed=25_000_000, transcendentals=2_000_000),
        name="project_and_convolve",
    )(slab, ends, x, w, gain, bias, taps, scale, shift)


def target_tables(data_group, lengths, assignment):
    count = lengths.shape[0]
    number = jnp.arange(count, dtype=jnp.int32)
    mine = assignment == data_group
    place = jnp.sum(jnp.where((number[None, :] < number[:, None]) & mine[None, :], 1, 0), axis=1)
    slot = jnp.arange(32, dtype=jnp.int32)
    spans = jnp.sum(jnp.where(mine[None, :] & (place[None, :] == slot[:, None]), lengths[None, :], 0), axis=1)
    first = jnp.sum(jnp.where(slot[None, :] < slot[:, None], spans[None, :], 0), axis=1)
    return first, first + spans


def on_device(
    query_rows,
    key_rows,
    value_rows,
    residual,
    lengths,
    assignment,
    out_proj,
    norm_gain,
    norm_bias,
    glu_proj,
    conv_taps,
    batch_scale,
    batch_shift,
    down_proj,
):
    data_group = lax.axis_index("dp").astype(jnp.int32)
    slab = lax.axis_index("mp").astype(jnp.int32)
    groups = lax.axis_size("dp")
    slabs = lax.axis_size("mp")
    part = lax.dynamic_slice(glu_proj.T, (48 * (data_group % 4), 768 * (data_group // 4)), (48, 768))
    op = lax.dynamic_slice(out_proj.T, (48 * (data_group % 2), 256 * (data_group // 2)), (48, 256))
    dn = lax.dynamic_slice(down_proj.T, (48 * (data_group % 2), 384 * (data_group // 2)), (48, 384))
    mine = jnp.concatenate([part, op, dn], axis=1)
    weights = lax.all_gather(mine, ("dp", "mp"), axis=0, tiled=True).reshape(groups, slabs, 48, 1408)

    group = data_group.reshape(1)
    x_cells = pack(group, lengths, assignment, residual.reshape(residual.shape[0], 384))
    x_here = lax.all_to_all(
        x_cells.reshape(groups, 4 * CELL, 384), "dp", split_axis=0, concat_axis=0, tiled=True
    )
    group_later, _ = lax.optimization_barrier((group, x_cells))
    c_cells = attend(
        group_later,
        lengths,
        assignment,
        query_rows.reshape(-1, 128),
        key_rows.reshape(-1, 128),
        value_rows.reshape(-1, 128),
    )
    x_here, first_cells = lax.optimization_barrier((x_here, c_cells[0]))
    c_here = [first_cells] + [
        lax.ppermute(c_cells[s], "dp", [(i, i ^ s) for i in range(groups)]) for s in range(1, groups)
    ]
    first, ends = target_tables(data_group, lengths, assignment)
    windows = compact(96, 0, group, first, [x_here.reshape(-1, 384)], slabs)
    windows = compact(64, 384, group, first, c_here, slabs, onto=windows)
    slab_rows = lax.all_to_all(windows, "mp", split_axis=0, concat_axis=0, tiled=True)
    row = lambda a: a.reshape(1, -1)
    return rest(
        slab.reshape(1),
        ends,
        slab_rows,
        weights,
        row(norm_gain),
        row(norm_bias),
        conv_taps,
        row(batch_scale),
        row(batch_shift),
    )


def solution(mesh):
    in_specs = (
        P("dp", "mp", None),
        P("dp", "mp", None),
        P("dp", "mp", None),
        P("dp", "mp", None),
        P(),
        P(),
        P(None, "mp"),
        P(),
        P(),
        P(None, "mp"),
        P(),
        P(),
        P(),
        P(None, "mp"),
    )
    out_specs = P(("dp", "mp"), None)
    return jax.shard_map(
        on_device, mesh=mesh, in_specs=in_specs, out_specs=out_specs, check_vma=False
    )
```

```python
import functools

import jax
import jax.numpy as jnp
from jax import lax
from jax.experimental import pallas as pl
from jax.experimental.pallas import tpu as pltpu
from jax.sharding import PartitionSpec as P

HD = 64
KERNEL = 31
HALF = 15
MAXLEN = 256
EPS = 1e-05
MASKED = -1e30

CELL = MAXLEN // 4
F32 = jnp.float32
BF16 = jnp.bfloat16
NT = (((1,), (1,)), ((), ()))


def cell_tables(data_group, lengths_ref, assignment_ref, start_ref, size_ref, seen_ref):
    per_group = 32
    for t in range(8):
        seen_ref[t] = 0

    def step(i, at):
        u = data_group * per_group + i
        t = assignment_ref[u]
        n = lengths_ref[u]
        k = seen_ref[t]
        seen_ref[t] = k + 1
        start_ref[4 * t + k] = at
        size_ref[4 * t + k] = n
        return at + n

    lax.fori_loop(0, per_group, step, jnp.int32(0))


def turn(x, s):
    return jnp.concatenate([x[:, s:], x[:, :s]], axis=1)


def pack_kernel(
    group_ref, lengths_ref, assignment_ref, x_ref, o_ref, flat, packed, start_ref, size_ref, seen_ref, sem
):
    cell_tables(group_ref[0], lengths_ref, assignment_ref, start_ref, size_ref, seen_ref)
    rows = x_ref.shape[0]

    def widen(i, _):
        r = pl.multiple_of(i * 64, 64)
        for b in range(3):
            flat[b, pl.ds(r, 64), :] = x_ref[pl.ds(r, 64), 128 * b : 128 * b + 128].astype(F32)
        return 0

    lax.fori_loop(0, rows // 64, widen, 0)
    for b in range(3):
        flat[b, rows : rows + 72, :] = jnp.zeros((72, 128), F32)
    lane = lax.broadcasted_iota(jnp.int32, (CELL, 384), 1)
    frame = 4 * lax.broadcasted_iota(jnp.int32, (CELL, 384), 0) + lane // 96

    def cell(c):
        b = start_ref[c]
        row = b // 4
        phase = b - 4 * row
        now = jnp.concatenate([flat[i, pl.ds(row, CELL), :] for i in range(3)], axis=1)
        later = jnp.concatenate([flat[i, pl.ds(row + 1, CELL), :] for i in range(3)], axis=1)
        mixed = jnp.where(lane >= 96 * phase, now, later)
        mixed = jnp.where(phase >= 2, turn(mixed, 192), mixed)
        mixed = jnp.where(phase % 2 == 1, turn(mixed, 96), mixed)
        return jnp.where(frame < size_ref[c], mixed, 0.0).astype(BF16)

    def target(t, _):
        parts = [cell(4 * t + k) for k in range(4)]
        at = pl.multiple_of(4 * CELL * t, 4 * CELL)
        for k, part in enumerate(parts):
            packed[pl.ds(at + k * CELL, CELL), :] = part
        pltpu.make_async_copy(packed.at[pl.ds(at, 4 * CELL), :], o_ref.at[pl.ds(at, 4 * CELL), :], sem).start()
        return 0

    lax.fori_loop(0, 8, target, 0)
    pltpu.make_async_copy(packed, o_ref, sem).wait()


def attend_kernel(
    group_ref, lengths_ref, assignment_ref, q_ref, k_ref, v_ref, *rest
):
    outs, (qf, kf, vf, o_ref, start_ref, size_ref, seen_ref, sem) = rest[:8], rest[8:]
    cell_tables(group_ref[0], lengths_ref, assignment_ref, start_ref, size_ref, seen_ref)
    rows = q_ref.shape[0]

    def widen(i, _):
        r = pl.multiple_of(i * 128, 128)
        qf[pl.ds(r, 128), :] = q_ref[pl.ds(r, 128), :].astype(F32) * (HD**-0.5)
        kf[pl.ds(r, 128), :] = k_ref[pl.ds(r, 128), :].astype(F32)
        vf[pl.ds(r, 128), :] = v_ref[pl.ds(r, 128), :].astype(F32)
        return 0

    lax.fori_loop(0, rows // 128, widen, 0)
    for ref in (qf, kf, vf):
        ref[rows : rows + 136, :] = jnp.zeros((136, 128), F32)
    lane = lax.broadcasted_iota(jnp.int32, (CELL, 128), 1)
    low = lane < 64
    frame = 4 * lax.broadcasted_iota(jnp.int32, (CELL, 128), 0) + lane // 64
    lane2 = lax.broadcasted_iota(jnp.int32, (2 * CELL, 128), 1)
    low2 = lane2 < 64
    column = lax.broadcasted_iota(jnp.int32, (1, MAXLEN), 1)
    key_frame = 2 * (column % 128) + column // 128

    def doubled(ref, row, shift):
        now = ref[pl.ds(row, 2 * CELL), :]
        later = ref[pl.ds(row + 1, 2 * CELL), :]
        even = jnp.where(lane2 >= shift, now, later)
        other = pltpu.roll(even, 64, 1)
        swap = shift > 0
        first = jnp.where(low2, even, other)
        second = jnp.where(low2, other, even)
        return jnp.concatenate(
            [jnp.where(swap, second, first), jnp.where(swap, first, second)], axis=0
        ).astype(BF16)

    def scored(c):
        b = start_ref[c]
        n = size_ref[c]
        row = b // 2
        shift = 64 * (b - 2 * row)
        u0 = qf[pl.ds(row, CELL, stride=2), :]
        u1 = qf[pl.ds(row + 1, CELL, stride=2), :]
        u2 = qf[pl.ds(row + 2, CELL, stride=2), :]
        v0 = pltpu.roll(jnp.where(lane >= shift, u0, u1), shift, 1)
        v1 = pltpu.roll(jnp.where(lane >= shift, u1, u2), shift, 1)
        queries = jnp.concatenate(
            [
                jnp.where(low, v0, 0.0),
                jnp.where(low, 0.0, v0),
                jnp.where(low, v1, 0.0),
                jnp.where(low, 0.0, v1),
            ],
            axis=0,
        ).astype(BF16)
        keys = doubled(kf, row, shift)
        values = doubled(vf, row, shift)
        return n, values, lax.dot_general(queries, keys, NT, preferred_element_type=F32)

    def weighted(n, scores):
        scores = jnp.where(key_frame < n, scores, MASKED)
        exponentials = jnp.exp(scores - jnp.max(scores, axis=1, keepdims=True))
        total = jnp.sum(exponentials, axis=1, keepdims=True)
        return exponentials.astype(BF16), total

    def store(c, n, values, exponentials, total):
        context = jnp.dot(exponentials, values, preferred_element_type=F32) * (1.0 / total)
        at = pl.multiple_of(c * CELL, CELL)
        first = jnp.where(low, context[0:64], context[64:128])
        second = jnp.where(low, context[128:192], context[192:256])
        o_ref[pl.ds(at, CELL), 0:128] = jnp.where(frame < n, first, 0.0).astype(BF16)
        o_ref[pl.ds(at, CELL), 128:256] = jnp.where(frame + 2 < n, second, 0.0).astype(BF16)

    def some(i, _):
        cells = [4 * i + c for c in range(4)]
        work = [scored(c) for c in cells]
        shares = [weighted(n, scores) for n, _, scores in work]
        for c, (n, values, _), share in zip(cells, work, shares):
            store(c, n, values, *share)
        return 0

    lax.fori_loop(0, 8, some, 0)
    copies = []
    for s in range(8):
        at = pl.multiple_of((group_ref[0] ^ s) * 4 * CELL, 4 * CELL)
        copies.append(pltpu.make_async_copy(o_ref.at[pl.ds(at, 4 * CELL), :], outs[s], sem.at[s]))
    for copy in copies:
        copy.start()
    for copy in copies:
        copy.wait()


def compact_kernel(width, offset, count, group_ref, after_ref, *rest):
    parts, (o_ref, flat, windows, sem) = rest[:count], rest[-4:]
    lanes = 4 * width
    blocks = lanes // 128
    total = flat.shape[1]
    slabs = o_ref.shape[0]

    def clear(i, _):
        r = pl.multiple_of(i * 16, 16)
        for b in range(blocks):
            flat[b, pl.ds(r, 16), :] = jnp.zeros((16, 128), F32)
        return 0

    lax.fori_loop(0, total // 16, clear, 0, unroll=7)
    lane = lax.broadcasted_iota(jnp.int32, (CELL, lanes), 1)

    def cell(block, first):
        row = first // 4
        phase = first - 4 * row
        block = block.astype(F32)
        block = jnp.where(phase >= 2, turn(block, lanes - 2 * width), block)
        block = jnp.where(phase % 2 == 1, turn(block, lanes - width), block)
        own = lane >= phase * width
        return row, jnp.where(own, block, 0.0), jnp.where(own, 0.0, block)

    def four(x_ref, at, u):
        moved = [cell(x_ref[pl.ds(at + k * CELL, CELL), :], after_ref[u + k]) for k in range(4)]
        for row, here, below in moved:
            for b in range(blocks):
                at = (b, pl.ds(row + 8, CELL), slice(None))
                flat[at] = flat[at] + here[:, 128 * b : 128 * b + 128]
            for b in range(blocks):
                at = (b, pl.ds(row + 9, CELL), slice(None))
                flat[at] = flat[at] + below[:, 128 * b : 128 * b + 128]

    if count == 1:

        def some(d, _):
            four(parts[0], pl.multiple_of(4 * CELL * d, 4 * CELL), 4 * d)
            return 0

        lax.fori_loop(0, 8, some, 0)
    else:
        for s, part in enumerate(parts):
            four(part, 0, 4 * (group_ref[0] ^ s))

    def window(m, _):
        for b in range(blocks):
            windows[m, :, 128 * b : 128 * b + 128] = flat[b, pl.ds(pl.multiple_of(m * 128, 128), 144), :].astype(BF16)
        pltpu.make_async_copy(windows.at[m], o_ref.at[m, :, pl.ds(offset, lanes)], sem).start()
        return 0

    lax.fori_loop(0, slabs, window, 0)
    pltpu.make_async_copy(windows, o_ref.at[:, :, pl.ds(offset, lanes)], sem).wait()


WIN = 144
EDGE = 8


def rest_kernel(
    slab_ref,
    ends_ref,
    r_ref,
    w_ref,
    gain_ref,
    bias_ref,
    taps_ref,
    scale_ref,
    shift_ref,
    o_ref,
    x_ref,
    wo,
    wg,
    wd,
    ctx,
    carried,
    normed,
    gated,
    segment,
    sums,
    swished,
    turned,
    sent,
    sems,
    xsems,
    osems,
):
    slab = slab_ref[0]
    arrived = []
    for q in range(4):
        part = (pl.ds(4 * q, 4), slice(None), slice(None))
        arrived.append(pltpu.make_async_copy(r_ref.at[part], x_ref.at[part], xsems.at[q]))
        arrived[q].start()
    wo3, wg3, wd3 = wo.reshape(16, 96, 1024), wg.reshape(16, 192, 1536), wd.reshape(16, 96, 1536)
    for c in range(2):
        for s in range(3):
            pltpu.make_async_copy(
                w_ref.at[c, :, pl.ds(0, 32), pl.ds(512 * s, 512)],
                wo3.at[:, pl.ds(32 * s, 32), pl.ds(512 * c, 512)],
                sems.at[0],
            ).start()
    for half in range(2):
        for first in (4 * half, 8 + 4 * half):
            for c in range(2):
                pltpu.make_async_copy(
                    w_ref.at[c, pl.ds(first, 4), pl.ds(32, 96), :],
                    wg3.at[pl.ds(first, 4), pl.ds(96 * c, 96), :],
                    sems.at[1 + half],
                ).start()
    for c in range(2):
        pltpu.make_async_copy(w_ref.at[c, :, pl.ds(128, 48), :], wd3.at[:, pl.ds(48 * c, 48), :], sems.at[3]).start()

    for j in range(4):
        frame = 512 * slab - 4 * EDGE + j + 4 * lax.broadcasted_iota(jnp.int32, (WIN, 128), 0)

        def count(i, number):
            return number + jnp.where(frame >= ends_ref[i], 1, 0)

        number = lax.fori_loop(0, 32, count, jnp.where(frame >= 0, 0, -1), unroll=4)
        segment[j] = number.astype(F32)

    for copy in arrived:
        copy.wait()
    lane = lax.broadcasted_iota(jnp.int32, (WIN, 384), 1)

    def features(g, _):
        at = pl.ds(pl.multiple_of(384 * g, 128), 384)
        for j in range(4):
            whole = None
            for f in range(4):
                s = 96 * ((f - j) % 4)
                block = x_ref[4 * g + f, :, 0:384]
                if s:
                    block = turn(block, 384 - s)
                whole = block if whole is None else jnp.where(lane >= 96 * f, block, whole)
            carried[WIN * j : WIN * j + WIN, at] = whole.astype(F32)
        return 0

    lax.fori_loop(0, 4, features, 0, unroll=2)

    low = lax.broadcasted_iota(jnp.int32, (WIN, 128), 1) < 64

    def heads(h, _):
        at = pl.ds(pl.multiple_of(128 * h, 128), 128)
        for j in range(4):
            part = slice(384 + 128 * (j // 2), 512 + 128 * (j // 2))
            left = x_ref[2 * h, :, part].astype(F32)
            right = x_ref[2 * h + 1, :, part].astype(F32)
            if j % 2 == 0:
                right = pltpu.roll(right, 64, 1)
            else:
                left = pltpu.roll(left, 64, 1)
            ctx[WIN * j : WIN * j + WIN, at] = jnp.where(low, left, right).astype(BF16)
        return 0

    lax.fori_loop(0, 8, heads, 0, unroll=4)

    pltpu.make_async_copy(wo, wo, sems.at[0]).wait()

    def project(n, _):
        at = pl.ds(pl.multiple_of(256 * n, 256), 256)
        carried[:, at] = carried[:, at] + lax.dot_general(
            ctx[...], wo[at, :], NT, preferred_element_type=F32
        )
        return 0

    lax.fori_loop(0, 6, project, 0, unroll=6)

    def norm(i, _):
        at = pl.ds(pl.multiple_of(16 * i, 16), 16)
        rows = carried[at, :]
        centred = rows - jnp.mean(rows, axis=1, keepdims=True)
        variance = jnp.mean(centred * centred, axis=1, keepdims=True)
        normed[at, :] = (centred * lax.rsqrt(variance + EPS) * gain_ref[...] + bias_ref[...]).astype(BF16)
        return 0

    lax.fori_loop(0, 4 * WIN // 16, norm, 0, unroll=6)

    def glu(n, _):
        value = lax.dot_general(
            normed[...], wg[pl.ds(pl.multiple_of(256 * n, 256), 256), :], NT, preferred_element_type=F32
        )
        gate = lax.dot_general(
            normed[...], wg[pl.ds(pl.multiple_of(1536 + 256 * n, 256), 256), :], NT, preferred_element_type=F32
        )
        out = (value * jax.nn.sigmoid(gate)).astype(BF16).astype(F32)
        for j in range(4):
            for b in range(2):
                gated[2 * n + b, j] = out[WIN * j : WIN * j + WIN, 128 * b : 128 * b + 128]
        return 0

    for half in range(2):
        part = wg.at[pl.ds(0, 1536), :]
        pltpu.make_async_copy(part, part, sems.at[1 + half]).wait()
        lax.fori_loop(3 * half, 3 * half + 3, glu, 0, unroll=3)

    def conv(b, _):
        lanes = [pl.ds(pl.multiple_of(512 * b + 128 * l, 128), 128) for l in range(4)]
        for first, last in ((-15, -8), (-7, 0), (1, 8), (9, 15)):
            taps = [
                {o: jnp.broadcast_to(taps_ref[o + HALF : o + HALF + 1, at], (8, 128)) for o in range(first, last + 1)}
                for at in lanes
            ]

            def chunk(i, _):
                row = EDGE + i * 8
                for pair in ((0, 1), (2, 3)):
                    mine = {j: segment[j, pl.ds(pl.multiple_of(row, 8), 8), :] for j in pair}
                    rows = {j: pl.ds(pl.multiple_of(128 * j + 8 * i, 8), 8) for j in pair}
                    total = {(l, j): None if first == -15 else sums[l, rows[j], :] for l in range(4) for j in pair}
                    for e in range(first + pair[0], last + pair[1] + 1):
                        d, p = e // 4, e % 4
                        values = [gated[4 * b + l, p, pl.ds(row + d, 8), :] for l in range(4)]
                        owner = segment[p, pl.ds(row + d, 8), :]
                        for j in pair:
                            if not first <= e - j <= last:
                                continue
                            same = owner == mine[j]
                            for l in range(4):
                                term = jnp.where(same, values[l], 0.0) * taps[l][e - j]
                                total[l, j] = term if total[l, j] is None else total[l, j] + term
                    for j in pair:
                        for l in range(4):
                            sums[l, rows[j], :] = total[l, j]
                return 0

            lax.fori_loop(0, 16, chunk, 0, unroll=2)
        for l, at in enumerate(lanes):
            affine = sums[l] * scale_ref[:, at] + shift_ref[:, at]
            swished[:, at] = (affine * jax.nn.sigmoid(affine)).astype(BF16)
        return 0

    lax.fori_loop(0, 3, conv, 0)

    pltpu.make_async_copy(wd, wd, sems.at[3]).wait()
    live = ends_ref[31]

    def down(n, _):
        at = pl.ds(pl.multiple_of(256 * n, 256), 256)
        lowered = lax.dot_general(swished[...], wd[at, :], NT, preferred_element_type=F32)
        for j in range(4):
            frame = 512 * slab + j + 4 * lax.broadcasted_iota(jnp.int32, (128, 256), 0)
            rows = carried[WIN * j + EDGE : WIN * j + EDGE + 128, at] + lowered[128 * j : 128 * j + 128]
            rows = jnp.where(frame < live, rows, 0.0)
            for b in range(2):
                turned[b, pl.ds(j, 128, stride=4), :] = rows[:, 128 * b : 128 * b + 128]
        sent[:, at] = jnp.concatenate([turned[0], turned[1]], axis=1).astype(BF16)
        pltpu.make_async_copy(sent.at[:, at], o_ref.at[:, at], osems.at[n]).start()
        return 0

    lax.fori_loop(0, 6, down, 0, unroll=6)
    for n in range(6):
        at = pl.ds(256 * n, 256)
        pltpu.make_async_copy(sent.at[:, at], o_ref.at[:, at], osems.at[n]).wait()


HBM = pl.BlockSpec(memory_space=pltpu.HBM)
SMEM = pl.BlockSpec(memory_space=pltpu.SMEM)
VMEM = pl.BlockSpec(memory_space=pltpu.VMEM)
BIG = 60 * 1024 * 1024


def pack(group, lengths, assignment, x):
    rows = x.shape[0]
    return pl.pallas_call(
        pack_kernel,
        out_shape=jax.ShapeDtypeStruct((32 * CELL, 384), BF16),
        in_specs=[SMEM, SMEM, SMEM, VMEM],
        out_specs=HBM,
        scratch_shapes=[
            pltpu.VMEM((3, rows + 72, 128), F32),
            pltpu.VMEM((32 * CELL, 384), BF16),
            pltpu.SMEM((32,), jnp.int32),
            pltpu.SMEM((32,), jnp.int32),
            pltpu.SMEM((8,), jnp.int32),
            pltpu.SemaphoreType.DMA,
        ],
        compiler_params=pltpu.CompilerParams(vmem_limit_bytes=24 * 1024 * 1024),
        cost_estimate=pl.CostEstimate(flops=20_000_000, bytes_accessed=3_200_000, transcendentals=0),
        name="pack_cells",
    )(group, lengths, assignment, x)


def attend(group, lengths, assignment, q, k, v):
    rows = q.shape[0]
    return pl.pallas_call(
        attend_kernel,
        out_shape=[jax.ShapeDtypeStruct((4 * CELL, 256), BF16)] * 8,
        in_specs=[SMEM, SMEM, SMEM, VMEM, VMEM, VMEM],
        out_specs=[HBM] * 8,
        scratch_shapes=[
            pltpu.VMEM((rows + 136, 128), F32),
            pltpu.VMEM((rows + 136, 128), F32),
            pltpu.VMEM((rows + 136, 128), F32),
            pltpu.VMEM((32 * CELL, 256), BF16),
            pltpu.SMEM((32,), jnp.int32),
            pltpu.SMEM((32,), jnp.int32),
            pltpu.SMEM((8,), jnp.int32),
            pltpu.SemaphoreType.DMA((8,)),
        ],
        compiler_params=pltpu.CompilerParams(vmem_limit_bytes=32 * 1024 * 1024),
        cost_estimate=pl.CostEstimate(flops=2_000_000_000, bytes_accessed=4_200_000, transcendentals=2_000_000),
        name="attend_cells",
    )(group, lengths, assignment, q, k, v)


def compact(width, offset, group, after, cells, slabs, onto=None):
    lanes = 4 * width
    return pl.pallas_call(
        functools.partial(compact_kernel, width, offset, len(cells)),
        out_shape=jax.ShapeDtypeStruct((slabs, WIN, 640), BF16),
        in_specs=[SMEM, SMEM] + [VMEM] * len(cells) + ([] if onto is None else [HBM]),
        out_specs=HBM,
        scratch_shapes=[
            pltpu.VMEM((lanes // 128, 32 * CELL + 80, 128), F32),
            pltpu.VMEM((slabs, WIN, lanes), BF16),
            pltpu.SemaphoreType.DMA,
        ],
        input_output_aliases={} if onto is None else {2 + len(cells): 0},
        compiler_params=pltpu.CompilerParams(vmem_limit_bytes=24 * 1024 * 1024),
        cost_estimate=pl.CostEstimate(flops=20_000_000, bytes_accessed=3_200_000, transcendentals=0),
        name="compact_cells",
    )(group, after, *cells, *([] if onto is None else [onto]))


def rest(slab, ends, x, w, gain, bias, taps, scale, shift):
    return pl.pallas_call(
        rest_kernel,
        out_shape=jax.ShapeDtypeStruct((512, 1536), BF16),
        in_specs=[SMEM, SMEM, HBM, HBM] + [VMEM] * 5,
        out_specs=HBM,
        scratch_shapes=[
            pltpu.VMEM((16, WIN, 640), BF16),
            pltpu.VMEM((1536, 1024), BF16),
            pltpu.VMEM((3072, 1536), BF16),
            pltpu.VMEM((1536, 1536), BF16),
            pltpu.VMEM((4 * WIN, 1024), BF16),
            pltpu.VMEM((4 * WIN, 1536), F32),
            pltpu.VMEM((4 * WIN, 1536), BF16),
            pltpu.VMEM((12, 4, WIN, 128), F32),
            pltpu.VMEM((4, WIN, 128), F32),
            pltpu.VMEM((4, 512, 128), F32),
            pltpu.VMEM((512, 1536), BF16),
            pltpu.VMEM((2, 512, 128), F32),
            pltpu.VMEM((512, 1536), BF16),
            pltpu.SemaphoreType.DMA((4,)),
            pltpu.SemaphoreType.DMA((4,)),
            pltpu.SemaphoreType.DMA((6,)),
        ],
        compiler_params=pltpu.CompilerParams(vmem_limit_bytes=BIG),
        cost_estimate=pl.CostEstimate(flops=9_000_000_000, bytes_accessed=25_000_000, transcendentals=2_000_000),
        name="project_and_convolve",
    )(slab, ends, x, w, gain, bias, taps, scale, shift)


def target_tables(data_group, lengths, assignment):
    count = lengths.shape[0]
    number = jnp.arange(count, dtype=jnp.int32)
    mine = assignment == data_group
    place = jnp.sum(jnp.where((number[None, :] < number[:, None]) & mine[None, :], 1, 0), axis=1)
    slot = jnp.arange(32, dtype=jnp.int32)
    spans = jnp.sum(jnp.where(mine[None, :] & (place[None, :] == slot[:, None]), lengths[None, :], 0), axis=1)
    first = jnp.sum(jnp.where(slot[None, :] < slot[:, None], spans[None, :], 0), axis=1)
    return first, first + spans


def on_device(
    query_rows,
    key_rows,
    value_rows,
    residual,
    lengths,
    assignment,
    out_proj,
    norm_gain,
    norm_bias,
    glu_proj,
    conv_taps,
    batch_scale,
    batch_shift,
    down_proj,
):
    data_group = lax.axis_index("dp").astype(jnp.int32)
    slab = lax.axis_index("mp").astype(jnp.int32)
    groups = lax.axis_size("dp")
    slabs = lax.axis_size("mp")
    core = data_group % 2
    op = lax.dynamic_slice_in_dim(out_proj.T, core * 512, 512, 1)
    op = jnp.concatenate([op[0:32], op[32:64], op[64:96]], axis=1)
    glu = lax.dynamic_slice_in_dim(glu_proj.T, core * 96, 96, 0)
    dn = lax.dynamic_slice_in_dim(down_proj.T, core * 48, 48, 0)
    mine = jnp.concatenate([op, glu, dn], axis=0)
    chips = [[(2 * p + c) * slabs + m for c in range(2) for m in range(slabs)] for p in range(groups // 2)]
    weights = lax.all_gather(mine, ("dp", "mp"), axis=0, tiled=True, axis_index_groups=chips).reshape(2, slabs, 176, 1536)

    group = data_group.reshape(1)
    x_cells = pack(group, lengths, assignment, residual.reshape(residual.shape[0], 384))
    x_here = lax.all_to_all(
        x_cells.reshape(groups, 4 * CELL, 384), "dp", split_axis=0, concat_axis=0, tiled=True
    )
    group_later, _ = lax.optimization_barrier((group, x_cells))
    c_cells = attend(
        group_later,
        lengths,
        assignment,
        query_rows.reshape(-1, 128),
        key_rows.reshape(-1, 128),
        value_rows.reshape(-1, 128),
    )
    x_here, first_cells = lax.optimization_barrier((x_here, c_cells[0]))
    c_here = [first_cells] + [
        lax.ppermute(c_cells[s], "dp", [(i, i ^ s) for i in range(groups)]) for s in range(1, groups)
    ]
    first, ends = target_tables(data_group, lengths, assignment)
    windows = compact(96, 0, group, first, [x_here.reshape(-1, 384)], slabs)
    windows = compact(64, 384, group, first, c_here, slabs, onto=windows)
    slab_rows = lax.all_to_all(windows, "mp", split_axis=0, concat_axis=0, tiled=True)
    row = lambda a: a.reshape(1, -1)
    return rest(
        slab.reshape(1),
        ends,
        slab_rows,
        weights,
        row(norm_gain),
        row(norm_bias),
        conv_taps,
        row(batch_scale),
        row(batch_shift),
    )


def solution(mesh):
    in_specs = (
        P("dp", "mp", None),
        P("dp", "mp", None),
        P("dp", "mp", None),
        P("dp", "mp", None),
        P(),
        P(),
        P(None, "mp"),
        P(),
        P(),
        P(None, "mp"),
        P(),
        P(),
        P(),
        P(None, "mp"),
    )
    out_specs = P(("dp", "mp"), None)
    return jax.shard_map(
        on_device, mesh=mesh, in_specs=in_specs, out_specs=out_specs, check_vma=False
    )
```

```python
import functools

import jax
import jax.numpy as jnp
from jax import lax
from jax.experimental import pallas as pl
from jax.experimental.pallas import tpu as pltpu
from jax.sharding import PartitionSpec as P

HD = 64
KERNEL = 31
HALF = 15
MAXLEN = 256
EPS = 1e-05
MASKED = -1e30

CELL = MAXLEN // 4
F32 = jnp.float32
BF16 = jnp.bfloat16
NT = (((1,), (1,)), ((), ()))


def cell_tables(data_group, lengths_ref, assignment_ref, start_ref, size_ref, seen_ref):
    per_group = 32
    for t in range(8):
        seen_ref[t] = 0

    def step(i, at):
        u = data_group * per_group + i
        t = assignment_ref[u]
        n = lengths_ref[u]
        k = seen_ref[t]
        seen_ref[t] = k + 1
        start_ref[4 * t + k] = at
        size_ref[4 * t + k] = n
        return at + n

    lax.fori_loop(0, per_group, step, jnp.int32(0))


def turn(x, s):
    return jnp.concatenate([x[:, s:], x[:, :s]], axis=1)


def pack_kernel(
    group_ref, lengths_ref, assignment_ref, x_ref, o_ref, flat, packed, start_ref, size_ref, seen_ref, sem
):
    cell_tables(group_ref[0], lengths_ref, assignment_ref, start_ref, size_ref, seen_ref)
    rows = x_ref.shape[0]

    def widen(i, _):
        r = pl.multiple_of(i * 64, 64)
        for b in range(3):
            flat[b, pl.ds(r, 64), :] = x_ref[pl.ds(r, 64), 128 * b : 128 * b + 128].astype(F32)
        return 0

    lax.fori_loop(0, rows // 64, widen, 0)
    for b in range(3):
        flat[b, rows : rows + 72, :] = jnp.zeros((72, 128), F32)
    lane = lax.broadcasted_iota(jnp.int32, (CELL, 384), 1)
    frame = 4 * lax.broadcasted_iota(jnp.int32, (CELL, 384), 0) + lane // 96

    def cell(c):
        b = start_ref[c]
        row = b // 4
        phase = b - 4 * row
        now = jnp.concatenate([flat[i, pl.ds(row, CELL), :] for i in range(3)], axis=1)
        later = jnp.concatenate([flat[i, pl.ds(row + 1, CELL), :] for i in range(3)], axis=1)
        mixed = jnp.where(lane >= 96 * phase, now, later)
        mixed = jnp.where(phase >= 2, turn(mixed, 192), mixed)
        mixed = jnp.where(phase % 2 == 1, turn(mixed, 96), mixed)
        return jnp.where(frame < size_ref[c], mixed, 0.0).astype(BF16)

    def target(t, _):
        parts = [cell(4 * t + k) for k in range(4)]
        at = pl.multiple_of(4 * CELL * t, 4 * CELL)
        for k, part in enumerate(parts):
            packed[pl.ds(at + k * CELL, CELL), :] = part
        pltpu.make_async_copy(packed.at[pl.ds(at, 4 * CELL), :], o_ref.at[pl.ds(at, 4 * CELL), :], sem).start()
        return 0

    lax.fori_loop(0, 8, target, 0)
    pltpu.make_async_copy(packed, o_ref, sem).wait()


def attend_kernel(
    group_ref, lengths_ref, assignment_ref, q_hbm, k_hbm, v_hbm, *rest
):
    outs, (q_ref, k_ref, v_ref, qf, kf, vf, o_ref, start_ref, size_ref, seen_ref, sem, arrivals) = rest[:8], rest[8:]
    inputs = [
        pltpu.make_async_copy(source, target, arrivals.at[i])
        for i, (source, target) in enumerate(((q_hbm, q_ref), (k_hbm, k_ref), (v_hbm, v_ref)))
    ]
    for copy in inputs:
        copy.start()
    cell_tables(group_ref[0], lengths_ref, assignment_ref, start_ref, size_ref, seen_ref)
    rows = q_ref.shape[0]
    for copy in inputs:
        copy.wait()

    def widen(i, _):
        r = pl.multiple_of(i * 128, 128)
        qf[pl.ds(r, 128), :] = q_ref[pl.ds(r, 128), :].astype(F32) * (HD**-0.5)
        kf[pl.ds(r, 128), :] = k_ref[pl.ds(r, 128), :].astype(F32)
        vf[pl.ds(r, 128), :] = v_ref[pl.ds(r, 128), :].astype(F32)
        return 0

    lax.fori_loop(0, rows // 128, widen, 0)
    for ref in (qf, kf, vf):
        ref[rows : rows + 136, :] = jnp.zeros((136, 128), F32)
    lane = lax.broadcasted_iota(jnp.int32, (CELL, 128), 1)
    low = lane < 64
    frame = 4 * lax.broadcasted_iota(jnp.int32, (CELL, 128), 0) + lane // 64
    lane2 = lax.broadcasted_iota(jnp.int32, (2 * CELL, 128), 1)
    low2 = lane2 < 64
    column = lax.broadcasted_iota(jnp.int32, (1, MAXLEN), 1)
    key_frame = 2 * (column % 128) + column // 128

    def doubled(ref, row, shift):
        now = ref[pl.ds(row, 2 * CELL), :]
        later = ref[pl.ds(row + 1, 2 * CELL), :]
        even = jnp.where(lane2 >= shift, now, later)
        other = pltpu.roll(even, 64, 1)
        swap = shift > 0
        first = jnp.where(low2, even, other)
        second = jnp.where(low2, other, even)
        return jnp.concatenate(
            [jnp.where(swap, second, first), jnp.where(swap, first, second)], axis=0
        ).astype(BF16)

    def scored(c):
        b = start_ref[c]
        n = size_ref[c]
        row = b // 2
        shift = 64 * (b - 2 * row)
        u0 = qf[pl.ds(row, CELL, stride=2), :]
        u1 = qf[pl.ds(row + 1, CELL, stride=2), :]
        u2 = qf[pl.ds(row + 2, CELL, stride=2), :]
        v0 = pltpu.roll(jnp.where(lane >= shift, u0, u1), shift, 1)
        v1 = pltpu.roll(jnp.where(lane >= shift, u1, u2), shift, 1)
        queries = jnp.concatenate(
            [
                jnp.where(low, v0, 0.0),
                jnp.where(low, 0.0, v0),
                jnp.where(low, v1, 0.0),
                jnp.where(low, 0.0, v1),
            ],
            axis=0,
        ).astype(BF16)
        keys = doubled(kf, row, shift)
        values = doubled(vf, row, shift)
        return n, values, lax.dot_general(queries, keys, NT, preferred_element_type=F32)

    def weighted(n, scores):
        scores = jnp.where(key_frame < n, scores, MASKED)
        exponentials = jnp.exp(scores - jnp.max(scores, axis=1, keepdims=True))
        total = jnp.sum(exponentials, axis=1, keepdims=True)
        return exponentials.astype(BF16), total

    def store(c, n, values, exponentials, total):
        context = jnp.dot(exponentials, values, preferred_element_type=F32) * (1.0 / total)
        at = pl.multiple_of(c * CELL, CELL)
        first = jnp.where(low, context[0:64], context[64:128])
        second = jnp.where(low, context[128:192], context[192:256])
        o_ref[pl.ds(at, CELL), 0:128] = jnp.where(frame < n, first, 0.0).astype(BF16)
        o_ref[pl.ds(at, CELL), 128:256] = jnp.where(frame + 2 < n, second, 0.0).astype(BF16)

    def some(i, _):
        cells = [4 * i + c for c in range(4)]
        work = [scored(c) for c in cells]
        shares = [weighted(n, scores) for n, _, scores in work]
        for c, (n, values, _), share in zip(cells, work, shares):
            store(c, n, values, *share)
        return 0

    lax.fori_loop(0, 8, some, 0)
    copies = []
    for s in range(8):
        at = pl.multiple_of((group_ref[0] ^ s) * 4 * CELL, 4 * CELL)
        copies.append(pltpu.make_async_copy(o_ref.at[pl.ds(at, 4 * CELL), :], outs[s], sem.at[s]))
    for copy in copies:
        copy.start()
    for copy in copies:
        copy.wait()


def compact_kernel(width, offset, count, group_ref, after_ref, *rest):
    parts, (o_ref, flat, windows, sem) = rest[:count], rest[-4:]
    lanes = 4 * width
    blocks = lanes // 128
    total = flat.shape[1]
    slabs = o_ref.shape[0]

    def clear(i, _):
        r = pl.multiple_of(i * 16, 16)
        for b in range(blocks):
            flat[b, pl.ds(r, 16), :] = jnp.zeros((16, 128), F32)
        return 0

    lax.fori_loop(0, total // 16, clear, 0, unroll=7)
    lane = lax.broadcasted_iota(jnp.int32, (CELL, lanes), 1)

    def cell(block, first):
        row = first // 4
        phase = first - 4 * row
        block = block.astype(F32)
        block = jnp.where(phase >= 2, turn(block, lanes - 2 * width), block)
        block = jnp.where(phase % 2 == 1, turn(block, lanes - width), block)
        own = lane >= phase * width
        return row, jnp.where(own, block, 0.0), jnp.where(own, 0.0, block)

    def four(x_ref, at, u):
        moved = [cell(x_ref[pl.ds(at + k * CELL, CELL), :], after_ref[u + k]) for k in range(4)]
        for row, here, below in moved:
            for b in range(blocks):
                at = (b, pl.ds(row + 8, CELL), slice(None))
                flat[at] = flat[at] + here[:, 128 * b : 128 * b + 128]
            for b in range(blocks):
                at = (b, pl.ds(row + 9, CELL), slice(None))
                flat[at] = flat[at] + below[:, 128 * b : 128 * b + 128]

    if count == 1:

        def some(d, _):
            four(parts[0], pl.multiple_of(4 * CELL * d, 4 * CELL), 4 * d)
            return 0

        lax.fori_loop(0, 8, some, 0)
    else:
        for s, part in enumerate(parts):
            four(part, 0, 4 * (group_ref[0] ^ s))

    def window(m, _):
        for b in range(blocks):
            windows[m, :, 128 * b : 128 * b + 128] = flat[b, pl.ds(pl.multiple_of(m * 128, 128), 144), :].astype(BF16)
        pltpu.make_async_copy(windows.at[m], o_ref.at[m, :, pl.ds(offset, lanes)], sem).start()
        return 0

    lax.fori_loop(0, slabs, window, 0)
    pltpu.make_async_copy(windows, o_ref.at[:, :, pl.ds(offset, lanes)], sem).wait()


WIN = 144
EDGE = 8


def rest_kernel(
    slab_ref,
    ends_ref,
    r_ref,
    w_ref,
    gain_ref,
    bias_ref,
    taps_ref,
    scale_ref,
    shift_ref,
    o_ref,
    x_ref,
    wo,
    wg,
    wd,
    ctx,
    carried,
    normed,
    gated,
    segment,
    sums,
    swished,
    turned,
    sent,
    sems,
    xsems,
    osems,
):
    slab = slab_ref[0]
    arrived = []
    for q in range(4):
        part = (pl.ds(4 * q, 4), slice(None), slice(None))
        arrived.append(pltpu.make_async_copy(r_ref.at[part], x_ref.at[part], xsems.at[q]))
        arrived[q].start()
    wo3, wg3, wd3 = wo.reshape(16, 96, 1024), wg.reshape(16, 192, 1536), wd.reshape(16, 96, 1536)
    for c in range(2):
        for s in range(3):
            pltpu.make_async_copy(
                w_ref.at[c, :, pl.ds(0, 32), pl.ds(512 * s, 512)],
                wo3.at[:, pl.ds(32 * s, 32), pl.ds(512 * c, 512)],
                sems.at[0],
            ).start()
    for half in range(2):
        for first in (4 * half, 8 + 4 * half):
            for c in range(2):
                pltpu.make_async_copy(
                    w_ref.at[c, pl.ds(first, 4), pl.ds(32, 96), :],
                    wg3.at[pl.ds(first, 4), pl.ds(96 * c, 96), :],
                    sems.at[1 + half],
                ).start()
    for c in range(2):
        pltpu.make_async_copy(w_ref.at[c, :, pl.ds(128, 48), :], wd3.at[:, pl.ds(48 * c, 48), :], sems.at[3]).start()

    for j in range(4):
        frame = 512 * slab - 4 * EDGE + j + 4 * lax.broadcasted_iota(jnp.int32, (WIN, 128), 0)

        def count(i, number):
            return number + jnp.where(frame >= ends_ref[i], 1, 0)

        number = lax.fori_loop(0, 32, count, jnp.where(frame >= 0, 0, -1), unroll=4)
        segment[j] = number.astype(F32)

    for copy in arrived:
        copy.wait()
    lane = lax.broadcasted_iota(jnp.int32, (WIN, 384), 1)

    def features(g, _):
        at = pl.ds(pl.multiple_of(384 * g, 128), 384)
        for j in range(4):
            whole = None
            for f in range(4):
                s = 96 * ((f - j) % 4)
                block = x_ref[4 * g + f, :, 0:384]
                if s:
                    block = turn(block, 384 - s)
                whole = block if whole is None else jnp.where(lane >= 96 * f, block, whole)
            carried[WIN * j : WIN * j + WIN, at] = whole.astype(F32)
        return 0

    lax.fori_loop(0, 4, features, 0, unroll=4)

    low = lax.broadcasted_iota(jnp.int32, (WIN, 128), 1) < 64

    def heads(h, _):
        at = pl.ds(pl.multiple_of(128 * h, 128), 128)
        for j in range(4):
            part = slice(384 + 128 * (j // 2), 512 + 128 * (j // 2))
            left = x_ref[2 * h, :, part].astype(F32)
            right = x_ref[2 * h + 1, :, part].astype(F32)
            if j % 2 == 0:
                right = pltpu.roll(right, 64, 1)
            else:
                left = pltpu.roll(left, 64, 1)
            ctx[WIN * j : WIN * j + WIN, at] = jnp.where(low, left, right).astype(BF16)
        return 0

    lax.fori_loop(0, 8, heads, 0, unroll=8)

    pltpu.make_async_copy(wo, wo, sems.at[0]).wait()

    def project(n, _):
        at = pl.ds(pl.multiple_of(256 * n, 256), 256)
        carried[:, at] = carried[:, at] + lax.dot_general(
            ctx[...], wo[at, :], NT, preferred_element_type=F32
        )
        return 0

    lax.fori_loop(0, 6, project, 0, unroll=6)

    def norm(i, _):
        at = pl.ds(pl.multiple_of(16 * i, 16), 16)
        rows = carried[at, :]
        centred = rows - jnp.mean(rows, axis=1, keepdims=True)
        variance = jnp.mean(centred * centred, axis=1, keepdims=True)
        normed[at, :] = (centred * lax.rsqrt(variance + EPS) * gain_ref[...] + bias_ref[...]).astype(BF16)
        return 0

    lax.fori_loop(0, 4 * WIN // 16, norm, 0, unroll=6)

    def glu(n, _):
        value = lax.dot_general(
            normed[...], wg[pl.ds(pl.multiple_of(256 * n, 256), 256), :], NT, preferred_element_type=F32
        )
        gate = lax.dot_general(
            normed[...], wg[pl.ds(pl.multiple_of(1536 + 256 * n, 256), 256), :], NT, preferred_element_type=F32
        )
        out = (value * jax.nn.sigmoid(gate)).astype(BF16).astype(F32)
        for j in range(4):
            for b in range(2):
                gated[2 * n + b, j] = out[WIN * j : WIN * j + WIN, 128 * b : 128 * b + 128]
        return 0

    for half in range(2):
        part = wg.at[pl.ds(0, 1536), :]
        pltpu.make_async_copy(part, part, sems.at[1 + half]).wait()
        lax.fori_loop(3 * half, 3 * half + 3, glu, 0, unroll=3)

    def conv(b, _):
        lanes = [pl.ds(pl.multiple_of(512 * b + 128 * l, 128), 128) for l in range(4)]
        for first, last in ((-15, -8), (-7, 0), (1, 8), (9, 15)):
            taps = [
                {o: jnp.broadcast_to(taps_ref[o + HALF : o + HALF + 1, at], (8, 128)) for o in range(first, last + 1)}
                for at in lanes
            ]

            def chunk(i, _):
                row = EDGE + i * 8
                for pair in ((0, 1), (2, 3)):
                    mine = {j: segment[j, pl.ds(pl.multiple_of(row, 8), 8), :] for j in pair}
                    rows = {j: pl.ds(pl.multiple_of(128 * j + 8 * i, 8), 8) for j in pair}
                    total = {(l, j): None if first == -15 else sums[l, rows[j], :] for l in range(4) for j in pair}
                    for e in range(first + pair[0], last + pair[1] + 1):
                        d, p = e // 4, e % 4
                        values = [gated[4 * b + l, p, pl.ds(row + d, 8), :] for l in range(4)]
                        owner = segment[p, pl.ds(row + d, 8), :]
                        for j in pair:
                            if not first <= e - j <= last:
                                continue
                            same = owner == mine[j]
                            for l in range(4):
                                term = jnp.where(same, values[l], 0.0) * taps[l][e - j]
                                total[l, j] = term if total[l, j] is None else total[l, j] + term
                    for j in pair:
                        for l in range(4):
                            sums[l, rows[j], :] = total[l, j]
                return 0

            lax.fori_loop(0, 16, chunk, 0, unroll=4)
        for l, at in enumerate(lanes):
            affine = sums[l] * scale_ref[:, at] + shift_ref[:, at]
            swished[:, at] = (affine * jax.nn.sigmoid(affine)).astype(BF16)
        return 0

    lax.fori_loop(0, 3, conv, 0)

    pltpu.make_async_copy(wd, wd, sems.at[3]).wait()
    live = ends_ref[31]

    def down(n, _):
        at = pl.ds(pl.multiple_of(256 * n, 256), 256)
        lowered = lax.dot_general(swished[...], wd[at, :], NT, preferred_element_type=F32)
        for j in range(4):
            frame = 512 * slab + j + 4 * lax.broadcasted_iota(jnp.int32, (128, 256), 0)
            rows = carried[WIN * j + EDGE : WIN * j + EDGE + 128, at] + lowered[128 * j : 128 * j + 128]
            rows = jnp.where(frame < live, rows, 0.0)
            for b in range(2):
                turned[b, pl.ds(j, 128, stride=4), :] = rows[:, 128 * b : 128 * b + 128]
        sent[:, at] = jnp.concatenate([turned[0], turned[1]], axis=1).astype(BF16)
        pltpu.make_async_copy(sent.at[:, at], o_ref.at[:, at], osems.at[n]).start()
        return 0

    lax.fori_loop(0, 6, down, 0, unroll=6)
    for n in range(6):
        at = pl.ds(256 * n, 256)
        pltpu.make_async_copy(sent.at[:, at], o_ref.at[:, at], osems.at[n]).wait()


HBM = pl.BlockSpec(memory_space=pltpu.HBM)
SMEM = pl.BlockSpec(memory_space=pltpu.SMEM)
VMEM = pl.BlockSpec(memory_space=pltpu.VMEM)
BIG = 60 * 1024 * 1024


def pack(group, lengths, assignment, x):
    rows = x.shape[0]
    return pl.pallas_call(
        pack_kernel,
        out_shape=jax.ShapeDtypeStruct((32 * CELL, 384), BF16),
        in_specs=[SMEM, SMEM, SMEM, VMEM],
        out_specs=HBM,
        scratch_shapes=[
            pltpu.VMEM((3, rows + 72, 128), F32),
            pltpu.VMEM((32 * CELL, 384), BF16),
            pltpu.SMEM((32,), jnp.int32),
            pltpu.SMEM((32,), jnp.int32),
            pltpu.SMEM((8,), jnp.int32),
            pltpu.SemaphoreType.DMA,
        ],
        compiler_params=pltpu.CompilerParams(vmem_limit_bytes=BIG),
        cost_estimate=pl.CostEstimate(flops=20_000_000, bytes_accessed=3_200_000, transcendentals=0),
        name="pack_cells",
    )(group, lengths, assignment, x)


def attend(group, lengths, assignment, q, k, v):
    rows = q.shape[0]
    return pl.pallas_call(
        attend_kernel,
        out_shape=[jax.ShapeDtypeStruct((4 * CELL, 256), BF16)] * 8,
        in_specs=[SMEM, SMEM, SMEM, HBM, HBM, HBM],
        out_specs=[HBM] * 8,
        scratch_shapes=[
            pltpu.VMEM((rows, 128), BF16),
            pltpu.VMEM((rows, 128), BF16),
            pltpu.VMEM((rows, 128), BF16),
            pltpu.VMEM((rows + 136, 128), F32),
            pltpu.VMEM((rows + 136, 128), F32),
            pltpu.VMEM((rows + 136, 128), F32),
            pltpu.VMEM((32 * CELL, 256), BF16),
            pltpu.SMEM((32,), jnp.int32),
            pltpu.SMEM((32,), jnp.int32),
            pltpu.SMEM((8,), jnp.int32),
            pltpu.SemaphoreType.DMA((8,)),
            pltpu.SemaphoreType.DMA((3,)),
        ],
        compiler_params=pltpu.CompilerParams(vmem_limit_bytes=BIG),
        cost_estimate=pl.CostEstimate(flops=2_000_000_000, bytes_accessed=4_200_000, transcendentals=2_000_000),
        name="attend_cells",
    )(group, lengths, assignment, q, k, v)


def compact(width, offset, group, after, cells, slabs, onto=None):
    lanes = 4 * width
    return pl.pallas_call(
        functools.partial(compact_kernel, width, offset, len(cells)),
        out_shape=jax.ShapeDtypeStruct((slabs, WIN, 640), BF16),
        in_specs=[SMEM, SMEM] + [VMEM] * len(cells) + ([] if onto is None else [HBM]),
        out_specs=HBM,
        scratch_shapes=[
            pltpu.VMEM((lanes // 128, 32 * CELL + 80, 128), F32),
            pltpu.VMEM((slabs, WIN, lanes), BF16),
            pltpu.SemaphoreType.DMA,
        ],
        input_output_aliases={} if onto is None else {2 + len(cells): 0},
        compiler_params=pltpu.CompilerParams(vmem_limit_bytes=24 * 1024 * 1024),
        cost_estimate=pl.CostEstimate(flops=20_000_000, bytes_accessed=3_200_000, transcendentals=0),
        name="compact_cells",
    )(group, after, *cells, *([] if onto is None else [onto]))


def rest(slab, ends, x, w, gain, bias, taps, scale, shift):
    return pl.pallas_call(
        rest_kernel,
        out_shape=jax.ShapeDtypeStruct((512, 1536), BF16),
        in_specs=[SMEM, SMEM, HBM, HBM] + [VMEM] * 5,
        out_specs=HBM,
        scratch_shapes=[
            pltpu.VMEM((16, WIN, 640), BF16),
            pltpu.VMEM((1536, 1024), BF16),
            pltpu.VMEM((3072, 1536), BF16),
            pltpu.VMEM((1536, 1536), BF16),
            pltpu.VMEM((4 * WIN, 1024), BF16),
            pltpu.VMEM((4 * WIN, 1536), F32),
            pltpu.VMEM((4 * WIN, 1536), BF16),
            pltpu.VMEM((12, 4, WIN, 128), F32),
            pltpu.VMEM((4, WIN, 128), F32),
            pltpu.VMEM((4, 512, 128), F32),
            pltpu.VMEM((512, 1536), BF16),
            pltpu.VMEM((2, 512, 128), F32),
            pltpu.VMEM((512, 1536), BF16),
            pltpu.SemaphoreType.DMA((4,)),
            pltpu.SemaphoreType.DMA((4,)),
            pltpu.SemaphoreType.DMA((6,)),
        ],
        compiler_params=pltpu.CompilerParams(vmem_limit_bytes=BIG),
        cost_estimate=pl.CostEstimate(flops=9_000_000_000, bytes_accessed=25_000_000, transcendentals=2_000_000),
        name="project_and_convolve",
    )(slab, ends, x, w, gain, bias, taps, scale, shift)


def target_tables(data_group, lengths, assignment):
    count = lengths.shape[0]
    number = jnp.arange(count, dtype=jnp.int32)
    mine = assignment == data_group
    place = jnp.sum(jnp.where((number[None, :] < number[:, None]) & mine[None, :], 1, 0), axis=1)
    slot = jnp.arange(32, dtype=jnp.int32)
    spans = jnp.sum(jnp.where(mine[None, :] & (place[None, :] == slot[:, None]), lengths[None, :], 0), axis=1)
    first = jnp.sum(jnp.where(slot[None, :] < slot[:, None], spans[None, :], 0), axis=1)
    return first, first + spans


def on_device(
    query_rows,
    key_rows,
    value_rows,
    residual,
    lengths,
    assignment,
    out_proj,
    norm_gain,
    norm_bias,
    glu_proj,
    conv_taps,
    batch_scale,
    batch_shift,
    down_proj,
):
    data_group = lax.axis_index("dp").astype(jnp.int32)
    slab = lax.axis_index("mp").astype(jnp.int32)
    groups = lax.axis_size("dp")
    slabs = lax.axis_size("mp")
    core = data_group % 2
    op = lax.dynamic_slice_in_dim(out_proj.T, core * 512, 512, 1)
    op = jnp.concatenate([op[0:32], op[32:64], op[64:96]], axis=1)
    glu = lax.dynamic_slice_in_dim(glu_proj.T, core * 96, 96, 0)
    dn = lax.dynamic_slice_in_dim(down_proj.T, core * 48, 48, 0)
    mine = jnp.concatenate([op, glu, dn], axis=0)
    chips = [[(2 * p + c) * slabs + m for c in range(2) for m in range(slabs)] for p in range(groups // 2)]
    weights = lax.all_gather(mine, ("dp", "mp"), axis=0, tiled=True, axis_index_groups=chips).reshape(2, slabs, 176, 1536)

    group = data_group.reshape(1)
    x_cells = pack(group, lengths, assignment, residual.reshape(residual.shape[0], 384))
    x_here = lax.all_to_all(
        x_cells.reshape(groups, 4 * CELL, 384), "dp", split_axis=0, concat_axis=0, tiled=True
    )
    group_later, _ = lax.optimization_barrier((group, x_cells))
    c_cells = attend(
        group_later,
        lengths,
        assignment,
        query_rows.reshape(-1, 128),
        key_rows.reshape(-1, 128),
        value_rows.reshape(-1, 128),
    )
    x_here, first_cells = lax.optimization_barrier((x_here, c_cells[0]))
    c_here = {0: first_cells}
    for s in (5, 4, 3, 7, 2, 6, 1):
        c_here[s] = lax.ppermute(c_cells[s], "dp", [(i, i ^ s) for i in range(groups)])
    c_here = [c_here[s] for s in range(groups)]
    first, ends = target_tables(data_group, lengths, assignment)
    windows = compact(96, 0, group, first, [x_here.reshape(-1, 384)], slabs)
    windows = compact(64, 384, group, first, c_here, slabs, onto=windows)
    slab_rows = lax.all_to_all(windows, "mp", split_axis=0, concat_axis=0, tiled=True)
    row = lambda a: a.reshape(1, -1)
    return rest(
        slab.reshape(1),
        ends,
        slab_rows,
        weights,
        row(norm_gain),
        row(norm_bias),
        conv_taps,
        row(batch_scale),
        row(batch_shift),
    )


def solution(mesh):
    in_specs = (
        P("dp", "mp", None),
        P("dp", "mp", None),
        P("dp", "mp", None),
        P("dp", "mp", None),
        P(),
        P(),
        P(None, "mp"),
        P(),
        P(),
        P(None, "mp"),
        P(),
        P(),
        P(),
        P(None, "mp"),
    )
    out_specs = P(("dp", "mp"), None)
    return jax.shard_map(
        on_device, mesh=mesh, in_specs=in_specs, out_specs=out_specs, check_vma=False
    )
```

```python
import functools

import jax
import jax.numpy as jnp
from jax import lax
from jax.experimental import pallas as pl
from jax.experimental.pallas import tpu as pltpu
from jax.sharding import PartitionSpec as P

HD = 64
KERNEL = 31
HALF = 15
MAXLEN = 256
EPS = 1e-05
MASKED = -1e30

CELL = MAXLEN // 4
F32 = jnp.float32
BF16 = jnp.bfloat16
NT = (((1,), (1,)), ((), ()))


def cell_tables(data_group, lengths_ref, assignment_ref, start_ref, size_ref, seen_ref):
    per_group = 32
    for t in range(8):
        seen_ref[t] = 0

    def step(i, at):
        u = data_group * per_group + i
        t = assignment_ref[u]
        n = lengths_ref[u]
        k = seen_ref[t]
        seen_ref[t] = k + 1
        start_ref[4 * t + k] = at
        size_ref[4 * t + k] = n
        return at + n

    lax.fori_loop(0, per_group, step, jnp.int32(0))


def turn(x, s):
    return jnp.concatenate([x[:, s:], x[:, :s]], axis=1)


def pack_kernel(
    group_ref, lengths_ref, assignment_ref, x_ref, o_ref, flat, packed, start_ref, size_ref, seen_ref, sem
):
    cell_tables(group_ref[0], lengths_ref, assignment_ref, start_ref, size_ref, seen_ref)
    rows = x_ref.shape[0]

    def widen(i, _):
        r = pl.multiple_of(i * 64, 64)
        for b in range(3):
            flat[b, pl.ds(r, 64), :] = x_ref[pl.ds(r, 64), 128 * b : 128 * b + 128].astype(F32)
        return 0

    lax.fori_loop(0, rows // 64, widen, 0)
    for b in range(3):
        flat[b, rows : rows + 72, :] = jnp.zeros((72, 128), F32)
    lane = lax.broadcasted_iota(jnp.int32, (CELL, 384), 1)
    frame = 4 * lax.broadcasted_iota(jnp.int32, (CELL, 384), 0) + lane // 96

    def cell(c):
        b = start_ref[c]
        row = b // 4
        phase = b - 4 * row
        now = jnp.concatenate([flat[i, pl.ds(row, CELL), :] for i in range(3)], axis=1)
        later = jnp.concatenate([flat[i, pl.ds(row + 1, CELL), :] for i in range(3)], axis=1)
        mixed = jnp.where(lane >= 96 * phase, now, later)
        mixed = jnp.where(phase >= 2, turn(mixed, 192), mixed)
        mixed = jnp.where(phase % 2 == 1, turn(mixed, 96), mixed)
        return jnp.where(frame < size_ref[c], mixed, 0.0).astype(BF16)

    def target(t, _):
        parts = [cell(4 * t + k) for k in range(4)]
        at = pl.multiple_of(4 * CELL * t, 4 * CELL)
        for k, part in enumerate(parts):
            packed[pl.ds(at + k * CELL, CELL), :] = part
        pltpu.make_async_copy(packed.at[pl.ds(at, 4 * CELL), :], o_ref.at[pl.ds(at, 4 * CELL), :], sem).start()
        return 0

    lax.fori_loop(0, 8, target, 0)
    pltpu.make_async_copy(packed, o_ref, sem).wait()


def attend_kernel(
    group_ref, lengths_ref, assignment_ref, q_hbm, k_hbm, v_hbm, *rest
):
    outs, (q_ref, k_ref, v_ref, qf, kf, vf, o_ref, start_ref, size_ref, seen_ref, sem, arrivals) = rest[:8], rest[8:]
    inputs = [
        pltpu.make_async_copy(source, target, arrivals.at[i])
        for i, (source, target) in enumerate(((q_hbm, q_ref), (k_hbm, k_ref), (v_hbm, v_ref)))
    ]
    for copy in inputs:
        copy.start()
    cell_tables(group_ref[0], lengths_ref, assignment_ref, start_ref, size_ref, seen_ref)
    rows = q_ref.shape[0]
    for copy in inputs:
        copy.wait()

    def widen(i, _):
        r = pl.multiple_of(i * 128, 128)
        qf[pl.ds(r, 128), :] = q_ref[pl.ds(r, 128), :].astype(F32) * (HD**-0.5)
        kf[pl.ds(r, 128), :] = k_ref[pl.ds(r, 128), :].astype(F32)
        vf[pl.ds(r, 128), :] = v_ref[pl.ds(r, 128), :].astype(F32)
        return 0

    lax.fori_loop(0, rows // 128, widen, 0)
    for ref in (qf, kf, vf):
        ref[rows : rows + 136, :] = jnp.zeros((136, 128), F32)
    lane = lax.broadcasted_iota(jnp.int32, (CELL, 128), 1)
    low = lane < 64
    frame = 4 * lax.broadcasted_iota(jnp.int32, (CELL, 128), 0) + lane // 64
    lane2 = lax.broadcasted_iota(jnp.int32, (2 * CELL, 128), 1)
    low2 = lane2 < 64
    column = lax.broadcasted_iota(jnp.int32, (1, MAXLEN), 1)
    key_frame = 2 * (column % 128) + column // 128

    def doubled(ref, row, shift):
        now = ref[pl.ds(row, 2 * CELL), :]
        later = ref[pl.ds(row + 1, 2 * CELL), :]
        even = jnp.where(lane2 >= shift, now, later)
        other = pltpu.roll(even, 64, 1)
        swap = shift > 0
        first = jnp.where(low2, even, other)
        second = jnp.where(low2, other, even)
        return jnp.concatenate(
            [jnp.where(swap, second, first), jnp.where(swap, first, second)], axis=0
        ).astype(BF16)

    def scored(c):
        b = start_ref[c]
        n = size_ref[c]
        row = b // 2
        shift = 64 * (b - 2 * row)
        u0 = qf[pl.ds(row, CELL, stride=2), :]
        u1 = qf[pl.ds(row + 1, CELL, stride=2), :]
        u2 = qf[pl.ds(row + 2, CELL, stride=2), :]
        v0 = pltpu.roll(jnp.where(lane >= shift, u0, u1), shift, 1)
        v1 = pltpu.roll(jnp.where(lane >= shift, u1, u2), shift, 1)
        queries = jnp.concatenate(
            [
                jnp.where(low, v0, 0.0),
                jnp.where(low, 0.0, v0),
                jnp.where(low, v1, 0.0),
                jnp.where(low, 0.0, v1),
            ],
            axis=0,
        ).astype(BF16)
        keys = doubled(kf, row, shift)
        values = doubled(vf, row, shift)
        return n, values, lax.dot_general(queries, keys, NT, preferred_element_type=F32)

    def weighted(n, scores):
        scores = jnp.where(key_frame < n, scores, MASKED)
        exponentials = jnp.exp(scores - jnp.max(scores, axis=1, keepdims=True))
        total = jnp.sum(exponentials, axis=1, keepdims=True)
        return exponentials.astype(BF16), total

    def store(c, n, values, exponentials, total):
        context = jnp.dot(exponentials, values, preferred_element_type=F32) * (1.0 / total)
        at = pl.multiple_of(c * CELL, CELL)
        first = jnp.where(low, context[0:64], context[64:128])
        second = jnp.where(low, context[128:192], context[192:256])
        o_ref[pl.ds(at, CELL), 0:128] = jnp.where(frame < n, first, 0.0).astype(BF16)
        o_ref[pl.ds(at, CELL), 128:256] = jnp.where(frame + 2 < n, second, 0.0).astype(BF16)

    def some(i, _):
        cells = [4 * i + c for c in range(4)]
        work = [scored(c) for c in cells]
        shares = [weighted(n, scores) for n, _, scores in work]
        for c, (n, values, _), share in zip(cells, work, shares):
            store(c, n, values, *share)
        return 0

    lax.fori_loop(0, 8, some, 0)
    copies = []
    for s in range(8):
        at = pl.multiple_of((group_ref[0] ^ s) * 4 * CELL, 4 * CELL)
        copies.append(pltpu.make_async_copy(o_ref.at[pl.ds(at, 4 * CELL), :], outs[s], sem.at[s]))
    for copy in copies:
        copy.start()
    for copy in copies:
        copy.wait()


def compact_kernel(width, offset, count, group_ref, after_ref, *rest):
    parts, (o_ref, flat, windows, sem) = rest[:count], rest[-4:]
    lanes = 4 * width
    blocks = lanes // 128
    total = flat.shape[1]
    slabs = o_ref.shape[0]

    def clear(i, _):
        r = pl.multiple_of(i * 16, 16)
        for b in range(blocks):
            flat[b, pl.ds(r, 16), :] = jnp.zeros((16, 128), F32)
        return 0

    lax.fori_loop(0, total // 16, clear, 0, unroll=7)
    lane = lax.broadcasted_iota(jnp.int32, (CELL, lanes), 1)

    def cell(block, first):
        row = first // 4
        phase = first - 4 * row
        block = block.astype(F32)
        block = jnp.where(phase >= 2, turn(block, lanes - 2 * width), block)
        block = jnp.where(phase % 2 == 1, turn(block, lanes - width), block)
        own = lane >= phase * width
        return row, jnp.where(own, block, 0.0), jnp.where(own, 0.0, block)

    def four(x_ref, at, u):
        moved = [cell(x_ref[pl.ds(at + k * CELL, CELL), :], after_ref[u + k]) for k in range(4)]
        for row, here, below in moved:
            for b in range(blocks):
                at = (b, pl.ds(row + 8, CELL), slice(None))
                flat[at] = flat[at] + here[:, 128 * b : 128 * b + 128]
            for b in range(blocks):
                at = (b, pl.ds(row + 9, CELL), slice(None))
                flat[at] = flat[at] + below[:, 128 * b : 128 * b + 128]

    if count == 1:

        def some(d, _):
            four(parts[0], pl.multiple_of(4 * CELL * d, 4 * CELL), 4 * d)
            return 0

        lax.fori_loop(0, 8, some, 0)
    else:
        for s, part in enumerate(parts):
            four(part, 0, 4 * (group_ref[0] ^ s))

    def window(m, _):
        for b in range(blocks):
            windows[m, :, 128 * b : 128 * b + 128] = flat[b, pl.ds(pl.multiple_of(m * 128, 128), 144), :].astype(BF16)
        pltpu.make_async_copy(windows.at[m], o_ref.at[m, :, pl.ds(offset, lanes)], sem).start()
        return 0

    lax.fori_loop(0, slabs, window, 0)
    pltpu.make_async_copy(windows, o_ref.at[:, :, pl.ds(offset, lanes)], sem).wait()


WIN = 144
EDGE = 8


def rest_kernel(
    slab_ref,
    ends_ref,
    r_ref,
    w_ref,
    gain_ref,
    bias_ref,
    taps_ref,
    scale_ref,
    shift_ref,
    o_ref,
    x_ref,
    wo,
    wg,
    wd,
    ctx,
    carried,
    normed,
    gated,
    segment,
    sums,
    swished,
    turned,
    sent,
    sems,
    xsems,
    osems,
):
    slab = slab_ref[0]
    arrived = []
    for q in range(4):
        part = (pl.ds(4 * q, 4), slice(None), slice(None))
        arrived.append(pltpu.make_async_copy(r_ref.at[part], x_ref.at[part], xsems.at[q]))
        arrived[q].start()
    wo3, wg3, wd3 = wo.reshape(16, 96, 1024), wg.reshape(16, 192, 1536), wd.reshape(16, 96, 1536)
    for c in range(2):
        for s in range(3):
            pltpu.make_async_copy(
                w_ref.at[c, :, pl.ds(0, 32), pl.ds(512 * s, 512)],
                wo3.at[:, pl.ds(32 * s, 32), pl.ds(512 * c, 512)],
                sems.at[0],
            ).start()
    for half in range(2):
        for first in (4 * half, 8 + 4 * half):
            for c in range(2):
                pltpu.make_async_copy(
                    w_ref.at[c, pl.ds(first, 4), pl.ds(32, 96), :],
                    wg3.at[pl.ds(first, 4), pl.ds(96 * c, 96), :],
                    sems.at[1 + half],
                ).start()
    for c in range(2):
        pltpu.make_async_copy(w_ref.at[c, :, pl.ds(128, 48), :], wd3.at[:, pl.ds(48 * c, 48), :], sems.at[3]).start()

    for j in range(4):
        frame = 512 * slab - 4 * EDGE + j + 4 * lax.broadcasted_iota(jnp.int32, (WIN, 128), 0)

        def count(i, number):
            return number + jnp.where(frame >= ends_ref[i], 1, 0)

        number = lax.fori_loop(0, 32, count, jnp.where(frame >= 0, 0, -1), unroll=4)
        segment[j] = number.astype(F32)

    lane = lax.broadcasted_iota(jnp.int32, (WIN, 384), 1)

    def features(g, _):
        at = pl.ds(pl.multiple_of(384 * g, 128), 384)
        for j in range(4):
            whole = None
            for f in range(4):
                s = 96 * ((f - j) % 4)
                block = x_ref[4 * g + f, :, 0:384]
                if s:
                    block = turn(block, 384 - s)
                whole = block if whole is None else jnp.where(lane >= 96 * f, block, whole)
            carried[WIN * j : WIN * j + WIN, at] = whole.astype(F32)
        return 0

    low = lax.broadcasted_iota(jnp.int32, (WIN, 128), 1) < 64

    def heads(h, _):
        at = pl.ds(pl.multiple_of(128 * h, 128), 128)
        for j in range(4):
            part = slice(384 + 128 * (j // 2), 512 + 128 * (j // 2))
            left = x_ref[2 * h, :, part].astype(F32)
            right = x_ref[2 * h + 1, :, part].astype(F32)
            if j % 2 == 0:
                right = pltpu.roll(right, 64, 1)
            else:
                left = pltpu.roll(left, 64, 1)
            ctx[WIN * j : WIN * j + WIN, at] = jnp.where(low, left, right).astype(BF16)
        return 0

    for q in range(4):
        arrived[q].wait()
        features(q, 0)
        heads(2 * q, 0)
        heads(2 * q + 1, 0)

    pltpu.make_async_copy(wo, wo, sems.at[0]).wait()

    def project(n, _):
        at = pl.ds(pl.multiple_of(256 * n, 256), 256)
        carried[:, at] = carried[:, at] + lax.dot_general(
            ctx[...], wo[at, :], NT, preferred_element_type=F32
        )
        return 0

    lax.fori_loop(0, 6, project, 0, unroll=6)

    def norm(i, _):
        at = pl.ds(pl.multiple_of(16 * i, 16), 16)
        rows = carried[at, :]
        centred = rows - jnp.mean(rows, axis=1, keepdims=True)
        variance = jnp.mean(centred * centred, axis=1, keepdims=True)
        normed[at, :] = (centred * lax.rsqrt(variance + EPS) * gain_ref[...] + bias_ref[...]).astype(BF16)
        return 0

    lax.fori_loop(0, 4 * WIN // 16, norm, 0, unroll=12)

    def glu(n, _):
        value = lax.dot_general(
            normed[...], wg[pl.ds(pl.multiple_of(256 * n, 256), 256), :], NT, preferred_element_type=F32
        )
        gate = lax.dot_general(
            normed[...], wg[pl.ds(pl.multiple_of(1536 + 256 * n, 256), 256), :], NT, preferred_element_type=F32
        )
        out = (value * jax.nn.sigmoid(gate)).astype(BF16).astype(F32)
        for j in range(4):
            for b in range(2):
                gated[2 * n + b, j] = out[WIN * j : WIN * j + WIN, 128 * b : 128 * b + 128]
        return 0

    for half in range(2):
        part = wg.at[pl.ds(0, 1536), :]
        pltpu.make_async_copy(part, part, sems.at[1 + half]).wait()
        lax.fori_loop(3 * half, 3 * half + 3, glu, 0, unroll=3)

    def conv(b, _):
        lanes = [pl.ds(pl.multiple_of(512 * b + 128 * l, 128), 128) for l in range(4)]
        for first, last in ((-15, -8), (-7, 0), (1, 8), (9, 15)):
            taps = [
                {o: jnp.broadcast_to(taps_ref[o + HALF : o + HALF + 1, at], (8, 128)) for o in range(first, last + 1)}
                for at in lanes
            ]

            def chunk(i, _):
                row = EDGE + i * 8
                for pair in ((0, 1), (2, 3)):
                    mine = {j: segment[j, pl.ds(pl.multiple_of(row, 8), 8), :] for j in pair}
                    rows = {j: pl.ds(pl.multiple_of(128 * j + 8 * i, 8), 8) for j in pair}
                    total = {(l, j): None if first == -15 else sums[l, rows[j], :] for l in range(4) for j in pair}
                    for e in range(first + pair[0], last + pair[1] + 1):
                        d, p = e // 4, e % 4
                        values = [gated[4 * b + l, p, pl.ds(row + d, 8), :] for l in range(4)]
                        owner = segment[p, pl.ds(row + d, 8), :]
                        for j in pair:
                            if not first <= e - j <= last:
                                continue
                            same = owner == mine[j]
                            for l in range(4):
                                term = jnp.where(same, values[l], 0.0) * taps[l][e - j]
                                total[l, j] = term if total[l, j] is None else total[l, j] + term
                    for j in pair:
                        for l in range(4):
                            sums[l, rows[j], :] = total[l, j]
                return 0

            lax.fori_loop(0, 16, chunk, 0, unroll=8)
        for l, at in enumerate(lanes):
            affine = sums[l] * scale_ref[:, at] + shift_ref[:, at]
            swished[:, at] = (affine * jax.nn.sigmoid(affine)).astype(BF16)
        return 0

    lax.fori_loop(0, 3, conv, 0)

    pltpu.make_async_copy(wd, wd, sems.at[3]).wait()
    live = ends_ref[31]

    def down(n, _):
        at = pl.ds(pl.multiple_of(256 * n, 256), 256)
        lowered = lax.dot_general(swished[...], wd[at, :], NT, preferred_element_type=F32)
        for j in range(4):
            frame = 512 * slab + j + 4 * lax.broadcasted_iota(jnp.int32, (128, 256), 0)
            rows = carried[WIN * j + EDGE : WIN * j + EDGE + 128, at] + lowered[128 * j : 128 * j + 128]
            rows = jnp.where(frame < live, rows, 0.0)
            for b in range(2):
                turned[b, pl.ds(j, 128, stride=4), :] = rows[:, 128 * b : 128 * b + 128]
        sent[:, at] = jnp.concatenate([turned[0], turned[1]], axis=1).astype(BF16)
        pltpu.make_async_copy(sent.at[:, at], o_ref.at[:, at], osems.at[n]).start()
        return 0

    lax.fori_loop(0, 6, down, 0, unroll=6)
    for n in range(6):
        at = pl.ds(256 * n, 256)
        pltpu.make_async_copy(sent.at[:, at], o_ref.at[:, at], osems.at[n]).wait()


HBM = pl.BlockSpec(memory_space=pltpu.HBM)
SMEM = pl.BlockSpec(memory_space=pltpu.SMEM)
VMEM = pl.BlockSpec(memory_space=pltpu.VMEM)
BIG = 60 * 1024 * 1024


def pack(group, lengths, assignment, x):
    rows = x.shape[0]
    return pl.pallas_call(
        pack_kernel,
        out_shape=jax.ShapeDtypeStruct((32 * CELL, 384), BF16),
        in_specs=[SMEM, SMEM, SMEM, VMEM],
        out_specs=HBM,
        scratch_shapes=[
            pltpu.VMEM((3, rows + 72, 128), F32),
            pltpu.VMEM((32 * CELL, 384), BF16),
            pltpu.SMEM((32,), jnp.int32),
            pltpu.SMEM((32,), jnp.int32),
            pltpu.SMEM((8,), jnp.int32),
            pltpu.SemaphoreType.DMA,
        ],
        compiler_params=pltpu.CompilerParams(vmem_limit_bytes=BIG),
        cost_estimate=pl.CostEstimate(flops=20_000_000, bytes_accessed=3_200_000, transcendentals=0),
        name="pack_cells",
    )(group, lengths, assignment, x)


def attend(group, lengths, assignment, q, k, v):
    rows = q.shape[0]
    return pl.pallas_call(
        attend_kernel,
        out_shape=[jax.ShapeDtypeStruct((4 * CELL, 256), BF16)] * 8,
        in_specs=[SMEM, SMEM, SMEM, HBM, HBM, HBM],
        out_specs=[HBM] * 8,
        scratch_shapes=[
            pltpu.VMEM((rows, 128), BF16),
            pltpu.VMEM((rows, 128), BF16),
            pltpu.VMEM((rows, 128), BF16),
            pltpu.VMEM((rows + 136, 128), F32),
            pltpu.VMEM((rows + 136, 128), F32),
            pltpu.VMEM((rows + 136, 128), F32),
            pltpu.VMEM((32 * CELL, 256), BF16),
            pltpu.SMEM((32,), jnp.int32),
            pltpu.SMEM((32,), jnp.int32),
            pltpu.SMEM((8,), jnp.int32),
            pltpu.SemaphoreType.DMA((8,)),
            pltpu.SemaphoreType.DMA((3,)),
        ],
        compiler_params=pltpu.CompilerParams(vmem_limit_bytes=BIG),
        cost_estimate=pl.CostEstimate(flops=2_000_000_000, bytes_accessed=4_200_000, transcendentals=2_000_000),
        name="attend_cells",
    )(group, lengths, assignment, q, k, v)


def compact(width, offset, group, after, cells, slabs, onto=None):
    lanes = 4 * width
    return pl.pallas_call(
        functools.partial(compact_kernel, width, offset, len(cells)),
        out_shape=jax.ShapeDtypeStruct((slabs, WIN, 640), BF16),
        in_specs=[SMEM, SMEM] + [VMEM] * len(cells) + ([] if onto is None else [HBM]),
        out_specs=HBM,
        scratch_shapes=[
            pltpu.VMEM((lanes // 128, 32 * CELL + 80, 128), F32),
            pltpu.VMEM((slabs, WIN, lanes), BF16),
            pltpu.SemaphoreType.DMA,
        ],
        input_output_aliases={} if onto is None else {2 + len(cells): 0},
        compiler_params=pltpu.CompilerParams(vmem_limit_bytes=24 * 1024 * 1024),
        cost_estimate=pl.CostEstimate(flops=20_000_000, bytes_accessed=3_200_000, transcendentals=0),
        name="compact_cells",
    )(group, after, *cells, *([] if onto is None else [onto]))


def rest(slab, ends, x, w, gain, bias, taps, scale, shift):
    return pl.pallas_call(
        rest_kernel,
        out_shape=jax.ShapeDtypeStruct((512, 1536), BF16),
        in_specs=[SMEM, SMEM, HBM, HBM] + [VMEM] * 5,
        out_specs=HBM,
        scratch_shapes=[
            pltpu.VMEM((16, WIN, 640), BF16),
            pltpu.VMEM((1536, 1024), BF16),
            pltpu.VMEM((3072, 1536), BF16),
            pltpu.VMEM((1536, 1536), BF16),
            pltpu.VMEM((4 * WIN, 1024), BF16),
            pltpu.VMEM((4 * WIN, 1536), F32),
            pltpu.VMEM((4 * WIN, 1536), BF16),
            pltpu.VMEM((12, 4, WIN, 128), F32),
            pltpu.VMEM((4, WIN, 128), F32),
            pltpu.VMEM((4, 512, 128), F32),
            pltpu.VMEM((512, 1536), BF16),
            pltpu.VMEM((2, 512, 128), F32),
            pltpu.VMEM((512, 1536), BF16),
            pltpu.SemaphoreType.DMA((4,)),
            pltpu.SemaphoreType.DMA((4,)),
            pltpu.SemaphoreType.DMA((6,)),
        ],
        compiler_params=pltpu.CompilerParams(vmem_limit_bytes=BIG),
        cost_estimate=pl.CostEstimate(flops=9_000_000_000, bytes_accessed=25_000_000, transcendentals=2_000_000),
        name="project_and_convolve",
    )(slab, ends, x, w, gain, bias, taps, scale, shift)


def target_tables(data_group, lengths, assignment):
    count = lengths.shape[0]
    number = jnp.arange(count, dtype=jnp.int32)
    mine = assignment == data_group
    place = jnp.sum(jnp.where((number[None, :] < number[:, None]) & mine[None, :], 1, 0), axis=1)
    slot = jnp.arange(32, dtype=jnp.int32)
    spans = jnp.sum(jnp.where(mine[None, :] & (place[None, :] == slot[:, None]), lengths[None, :], 0), axis=1)
    first = jnp.sum(jnp.where(slot[None, :] < slot[:, None], spans[None, :], 0), axis=1)
    return first, first + spans


def on_device(
    query_rows,
    key_rows,
    value_rows,
    residual,
    lengths,
    assignment,
    out_proj,
    norm_gain,
    norm_bias,
    glu_proj,
    conv_taps,
    batch_scale,
    batch_shift,
    down_proj,
):
    data_group = lax.axis_index("dp").astype(jnp.int32)
    slab = lax.axis_index("mp").astype(jnp.int32)
    groups = lax.axis_size("dp")
    slabs = lax.axis_size("mp")
    core = data_group % 2
    op = lax.dynamic_slice_in_dim(out_proj.T, core * 512, 512, 1)
    op = jnp.concatenate([op[0:32], op[32:64], op[64:96]], axis=1)
    glu = lax.dynamic_slice_in_dim(glu_proj.T, core * 96, 96, 0)
    dn = lax.dynamic_slice_in_dim(down_proj.T, core * 48, 48, 0)
    mine = jnp.concatenate([op, glu, dn], axis=0)
    chips = [[(2 * p + c) * slabs + m for c in range(2) for m in range(slabs)] for p in range(groups // 2)]
    weights = lax.all_gather(mine, ("dp", "mp"), axis=0, tiled=True, axis_index_groups=chips).reshape(2, slabs, 176, 1536)

    group = data_group.reshape(1)
    x_cells = pack(group, lengths, assignment, residual.reshape(residual.shape[0], 384))
    x_here = lax.all_to_all(
        x_cells.reshape(groups, 4 * CELL, 384), "dp", split_axis=0, concat_axis=0, tiled=True
    )
    group_later, _ = lax.optimization_barrier((group, x_cells))
    c_cells = attend(
        group_later,
        lengths,
        assignment,
        query_rows.reshape(-1, 128),
        key_rows.reshape(-1, 128),
        value_rows.reshape(-1, 128),
    )
    x_here, first_cells = lax.optimization_barrier((x_here, c_cells[0]))
    c_here = {0: first_cells}
    for s in (5, 4, 3, 7, 2, 6, 1):
        c_here[s] = lax.ppermute(c_cells[s], "dp", [(i, i ^ s) for i in range(groups)])
    c_here = [c_here[s] for s in range(groups)]
    first, ends = target_tables(data_group, lengths, assignment)
    windows = compact(96, 0, group, first, [x_here.reshape(-1, 384)], slabs)
    windows = compact(64, 384, group, first, c_here, slabs, onto=windows)
    slab_rows = lax.all_to_all(windows, "mp", split_axis=0, concat_axis=0, tiled=True)
    row = lambda a: a.reshape(1, -1)
    return rest(
        slab.reshape(1),
        ends,
        slab_rows,
        weights,
        row(norm_gain),
        row(norm_bias),
        conv_taps,
        row(batch_scale),
        row(batch_shift),
    )


def solution(mesh):
    in_specs = (
        P("dp", "mp", None),
        P("dp", "mp", None),
        P("dp", "mp", None),
        P("dp", "mp", None),
        P(),
        P(),
        P(None, "mp"),
        P(),
        P(),
        P(None, "mp"),
        P(),
        P(),
        P(),
        P(None, "mp"),
    )
    out_specs = P(("dp", "mp"), None)
    return jax.shard_map(
        on_device, mesh=mesh, in_specs=in_specs, out_specs=out_specs, check_vma=False
    )
```
